256 devices in a mesh: sec: 4 (over x_lo, core), dev: 64 (over x_hi, z, y).
Axes of the slice: x: 4 (x_hi: 2, x_lo: 2; x = x_hi * 2 + x_lo), y: 4, z: 8, core: 2. Of those that a mesh axis runs over, the one named last changes fastest.
Arguments:
- queries: bfloat16 [256, 128, 576], P(('sec', 'dev')), may hold values from -56 to 56
- latent_cache: bfloat16 [256, 4096, 576], P(('sec', 'dev')), may hold values from -4 to 4
- cache_lengths: int32 [256], P(('sec', 'dev')), may hold values from 512 to 4096, as said below
- stream: bfloat16 [512, 7168], P('dev'), may hold values from -6 to 6
- norm_gain: float32 [7168], replicated, may hold values from 0.1 to 1.9
- expert_ids: int32 [512, 8], P('dev'), may hold values from 0 to 15, all different within a row; in each aligned block of 8 rows (0 to 7, 8 to 15, ...) at most 5 rows name the same one
- route_weights: float32 [512, 8], P('dev'), may hold values from 0.1 to 1
- w_gate: bfloat16 [64, 7168, 512], P('dev', None, 'sec'), may hold values from -0.0625 to 0.0625
- w_up: bfloat16 [64, 7168, 512], P('dev', None, 'sec'), may hold values from -0.0625 to 0.0625
- w_down: bfloat16 [64, 512, 7168], P('dev', 'sec'), may hold values from -0.125 to 0.125
Outputs:
- context: bfloat16 [256, 128, 512], P(('sec', 'dev'))
- mixed: bfloat16 [512, 7168], P('dev')
The draws below stay inside these ranges and needn't reach their ends.
Inputs may be any that keep to these rules, and one draw needn't show every extreme that they name: `expert_ids`: each row names 8 distinct experts; within the 8 rows of one group no expert is named more than 5 times, a bound that some block reaches. `cache_lengths`: the longest sequence holds 4096 positions.
All inputs are finite; a program needn't handle non-finite values.
Results may differ from the reference program's by a relative error of at most 0.015.
Values may be sent and summed in bfloat16 or wider, within the bound.
No kernel may reach another device: no remote copies, remote signals or barrier semaphores. Data moves between devices by JAX's collectives and lax.ppermute only.
A program may use at most 128 MiB of HBM per device.

```python
import math
import jax
import jax.numpy as jnp
import numpy as np
from jax import lax

D = 7168
MOE_HIDDEN = 2048
HEADS = 128
LATENT = 512
ROPE = 64
HID_DEV = 128
CACHE_LEN = 4096
ROWS_DEV = 8
SEC_UNITS = 512
GROUP = 4
EXPERTS = 16
TOPK = 8
CAP = 5
SEQS = 256
MOE_ROWS = 512
N_SEC = 4
N_DEV = 64


def key_table(key):
    subkey = jax.random.fold_in(key, 101)
    values_raw = jax.random.normal(subkey, (SEQS, CACHE_LEN, LATENT + ROPE), jnp.float32)
    return jnp.clip(values_raw, -4.0, 4.0)


def length_table(key):
    subkey = jax.random.fold_in(key, 202)
    valid_len = jax.random.randint(subkey, (SEQS,), CACHE_LEN // 8, CACHE_LEN + 1)
    longest = jax.random.randint(jax.random.fold_in(subkey, 7), (), 0, SEQS)
    return valid_len.at[longest].set(CACHE_LEN).astype(jnp.int32)


def draw_cache_lengths(key, part):
    return length_table(key)


def draw_latent_cache(key, part):
    table = key_table(key)
    return table.astype(jnp.bfloat16)


def draw_queries(key, part):
    key = jax.random.fold_in(key, 3)
    result = jnp.clip(jax.random.normal(key, (SEQS, HEADS, LATENT + ROPE), jnp.float32), -4.0, 4.0)
    return result.astype(jnp.bfloat16)


def block_levels(rng, dims, split, low, top_value):
    def one(dim, parts):
        heights = jax.random.uniform(jax.random.fold_in(jax.random.fold_in(rng, 6), dim), (parts,), jnp.float32, low / len(split), top_value / len(split))
        return jnp.repeat(jnp.exp(heights), dims[dim] // parts).reshape((-1,) + (1,) * (len(dims) - dim - 1))

    gain = one(*split[0])
    for cut in split[1:]:
        gain = gain * one(*cut)
    return gain


def assign_block(own_key, own, number, rows, count, top, bound, slope):
    sequence = jax.random.permutation(own_key, count)
    crowded, usual = shares(count, rows * top, bound, slope, True), shares(count, rows * top, bound, slope, False)
    places = jnp.arange(count)

    def named(lengths, rotation):
        used = int((lengths > 0).sum())
        fixed = max(1, used // 4)
        shifted = fixed + (places - fixed + rotation * (used - fixed)) % max(1, count - fixed)
        return jnp.zeros((count,), jnp.int32).at[sequence[jnp.where(places < fixed, places, shifted)]].set(jnp.asarray(lengths, jnp.int32))

    lengths = jnp.where(number % 4 == 0, named(crowded, number // 4), named(usual, number - number // 4 - 1))
    mixed = jax.random.permutation(jax.random.fold_in(own, 3), count)
    source_of, taker = mixed[0:count // 2 * 2:2], mixed[1:count // 2 * 2:2]
    slack = jnp.minimum(lengths[source_of] - 1, bound - lengths[taker]) // 2
    slack = jnp.where((source_of == sequence[0]) | (taker == sequence[0]) | (lengths[taker] == 0), 0, jnp.maximum(slack, 0))
    shifted = jax.random.randint(jax.random.fold_in(own, 4), (count // 2,), 0, 1 << 20) % (slack + 1)
    lengths = lengths.at[source_of].add(-shifted).at[taker].add(shifted)
    items = jnp.searchsorted(jnp.cumsum(lengths), jnp.arange(rows * top), side="right").astype(jnp.int32)
    listing = items.reshape(top, rows).T
    listing = listing[jax.random.permutation(jax.random.fold_in(own, 1), rows)]
    rotation = jax.random.randint(jax.random.fold_in(own, 2), (rows, 1), 0, top)
    return jnp.take_along_axis(listing, (jnp.arange(top)[None, :] + rotation) % top, axis=1)


def shares(amount, total, limit, skew, full):
    loads = [(1 << 20) // math.isqrt(rank ** skew) + 1 for rank in range(1, amount + 1)]
    largest = limit if full else min(limit, max(-(-total // amount), total * loads[0] // sum(loads)))
    least = 1 if total - largest >= amount - 1 else 0
    counts, spare = [largest] + [least] * (amount - 1), total - largest - least * (amount - 1)
    while spare > 0:
        candidates = [i for i in range(1, amount) if counts[i] < largest] or [i for i in range(1, amount) if counts[i] < limit]
        whole, remaining = sum([loads[i] for i in candidates]), spare
        for i in candidates:
            more = min(limit - counts[i], max(1, remaining * loads[i] // whole), spare)
            counts[i] = counts[i] + more
            spare = spare - more
    return np.array(counts)


def gaussian(rng, dims, width, limit, cuts=(), held_as=jnp.bfloat16):
    level = block_levels(rng, dims, cuts, -0.22, 0.18) if cuts else 1.0
    values = jax.random.normal(rng, dims, jnp.float32) * width * level
    return jnp.minimum(jnp.maximum(values, -limit), limit).astype(held_as)


def setup_inputs(seed: int = 0) -> dict:
    splits = jax.random.split(jax.random.key(seed), 11)
    queries = draw_queries(jax.random.fold_in(splits[10], 71), 0)
    latent_cache = draw_latent_cache(jax.random.fold_in(splits[10], 71), 0)
    cache_lengths = draw_cache_lengths(jax.random.fold_in(splits[10], 71), 0)
    stream = gaussian(splits[3], (MOE_ROWS, D), 1.0, 6.0, ((0, 64),))
    norm_gain = jnp.clip(1.0 + 0.18 * jax.random.normal(splits[4], (D,), jnp.float32), 0.1, 1.9)
    expert_ids_keys = jax.random.split(jax.random.fold_in(splits[5], 1), MOE_ROWS // ROWS_DEV)
    expert_ids_turns = jax.random.permutation(jax.random.fold_in(splits[5], 3), MOE_ROWS // ROWS_DEV)
    expert_ids = jax.vmap(lambda own, number: assign_block(jax.random.fold_in(splits[5], 2), own, number, ROWS_DEV, EXPERTS, TOPK, CAP, 1))(expert_ids_keys, expert_ids_turns).reshape((MOE_ROWS, TOPK))
    route_weights = jnp.clip(jnp.exp(math.log(1.0) - 2.3025851 * jax.random.uniform(splits[6], (MOE_ROWS, TOPK), jnp.float32) ** block_levels(splits[6], (MOE_ROWS, TOPK), ((0, 64),), -0.2, 0.2)), 0.1, 1.0)
    w_gate = gaussian(splits[7], (N_DEV, D, SEC_UNITS), D ** -0.5, 0.0625, ((0, 64), (2, 4)))
    w_up = gaussian(splits[8], (N_DEV, D, SEC_UNITS), D ** -0.5, 0.0625, ((0, 64), (2, 4)))
    w_down = gaussian(splits[9], (N_DEV, SEC_UNITS, D), MOE_HIDDEN ** -0.5, 0.125, ((0, 64), (1, 4)))
    return dict(queries=queries, latent_cache=latent_cache, cache_lengths=cache_lengths, stream=stream, norm_gain=norm_gain, expert_ids=expert_ids, route_weights=route_weights, w_gate=w_gate, w_up=w_up, w_down=w_down)


score_scale = 192.0 ** (-0.5)

def slot_table(choices, count, capacity):
    experts = jnp.arange(count, dtype=jnp.int32)
    hit_count = lax.optimization_barrier(jnp.sum((choices[..., None] == experts).astype(jnp.float32), axis=2))
    before = jnp.cumsum(hit_count, axis=1) - hit_count
    slot_ids = jnp.arange(capacity).astype(jnp.float32)
    picked = hit_count[..., None] * (before[..., None] == slot_ids).astype(jnp.float32)
    return (jnp.transpose(picked, (0, 2, 3, 1)), hit_count)

def attend_one(items):
    query_rows, cache_rows, valid_len = items
    scores = jnp.dot(query_rows, cache_rows.T, preferred_element_type=jnp.float32) * score_scale
    visible = jnp.arange(cache_rows.shape[0], dtype=jnp.int32)[None, :] < valid_len
    scores = jnp.where(visible, scores, jnp.float32(-1e+30))
    peak = lax.optimization_barrier(jnp.max(scores, axis=1, keepdims=True))
    powered = jnp.exp(scores - peak)
    probs = (powered / lax.optimization_barrier(jnp.sum(powered, axis=1, keepdims=True))).astype(jnp.bfloat16)
    return jnp.dot(probs, cache_rows[:, :LATENT], preferred_element_type=jnp.float32).astype(jnp.bfloat16)

def expert_one(items):
    rows_in, gate_w, up_w, down_w = items
    rows_f = rows_in.astype(jnp.float32)
    gate_proj = jnp.einsum('md,pdc->mpc', rows_f, gate_w.astype(jnp.float32))
    up_proj = jnp.einsum('md,pdc->mpc', rows_f, up_w.astype(jnp.float32))
    hidden = (jax.nn.silu(gate_proj) * up_proj).astype(jnp.bfloat16)
    hidden = hidden.reshape(rows_in.shape[0], GROUP, N_SEC, HID_DEV)
    down_split = down_w.reshape(GROUP, N_SEC, HID_DEV, D)
    partial_value = jnp.einsum('mpsk,pskd->mpsd', hidden.astype(jnp.float32), down_split.astype(jnp.float32)).astype(jnp.bfloat16)
    return lax.optimization_barrier(jnp.sum(partial_value.astype(jnp.float32), axis=(1, 2)))

def reference(queries, latent_cache, cache_lengths, stream, norm_gain, expert_ids, route_weights, w_gate, w_up, w_down):
    context = lax.map(attend_one, (queries, latent_cache, cache_lengths))
    stream_f = stream.astype(jnp.float32)
    scale_rows = lax.rsqrt(lax.optimization_barrier(jnp.mean(stream_f * stream_f, axis=1, keepdims=True)) + 1e-06)
    normed = (stream_f * scale_rows * norm_gain).astype(jnp.bfloat16)
    groups = N_DEV
    choices = expert_ids.reshape(groups, ROWS_DEV, TOPK)
    picked, hit_count = slot_table(choices, EXPERTS, CAP)
    rows_grouped = normed.reshape(groups, ROWS_DEV, D)
    slot_rows = jnp.einsum('gejr,grd->gejd', picked, rows_grouped.astype(jnp.float32)).astype(jnp.bfloat16)
    expert_rows = jnp.transpose(slot_rows, (1, 0, 2, 3)).reshape(EXPERTS, groups * CAP, D)
    gate_all = w_gate.reshape(EXPERTS, GROUP, D, SEC_UNITS)
    up_all = w_up.reshape(EXPERTS, GROUP, D, SEC_UNITS)
    down_all = w_down.reshape(EXPERTS, GROUP, SEC_UNITS, D)
    expert_out = lax.map(expert_one, (expert_rows, gate_all, up_all, down_all))
    expert_out = expert_out.reshape(EXPERTS, groups, CAP, D)
    weights_grouped = route_weights.reshape(groups, ROWS_DEV, TOPK)
    experts = jnp.arange(EXPERTS, dtype=jnp.int32)
    weight_table = lax.optimization_barrier(jnp.sum(weights_grouped[..., None] * (choices[..., None] == experts).astype(jnp.float32), axis=2))
    weighted = picked * jnp.transpose(weight_table, (0, 2, 1))[:, :, None, :]
    moe = jnp.einsum('gejr,egjd->grd', weighted, expert_out, precision=lax.Precision.HIGHEST)
    mixed = (stream_f + moe.reshape(groups * ROWS_DEV, D)).astype(jnp.bfloat16)
    return (context, mixed)
```

```python
import functools

import jax
import jax.numpy as jnp
from jax import lax
from jax.experimental import pallas as pl
from jax.experimental.pallas import tpu as pltpu
from jax.sharding import PartitionSpec as P

LATENT = 512
CAP = 5
ROWS = 8
WIDTH = 7168
HALF = 3584
SLOTS = 40
score_scale = 192.0 ** (-0.5)

SIZES = (2, 2, 2, 8, 4)


def pairs(move):
    out = []
    for xl in range(2):
        for c in range(2):
            for xh in range(2):
                for z in range(8):
                    for y in range(4):
                        place = (xl, c, xh, z, y)
                        lin = []
                        for spot in (place, move(*place)):
                            at = 0
                            for part, size in zip(spot, SIZES):
                                at = at * size + part % size
                            lin.append(at)
                        out.append(tuple(lin))
    return out


def send(value, move):
    return lax.ppermute(value, ("sec", "dev"), pairs(move))


def swap_core(value):
    return send(value, lambda xl, c, xh, z, y: (xl, 1 - c, xh, z, y))


def z_step(c, k):
    return k if c == 0 else -(k + 1)


def spread(value, k, sign):
    return send(
        value, lambda xl, c, xh, z, y: (xl, c, xh ^ xl, z + sign * z_step(c, k), y)
    )


def across(value, dxl, dy):
    return send(value, lambda xl, c, xh, z, y: (xl ^ dxl, c, xh, z, y + dy))


ORDER = (3, 2, 1, 0)
DELTAS = ((1, 2), (1, 1), (1, 3), (0, 2), (0, 1), (0, 3), (1, 0))


def pick_kernel(at_ref, r0, r1, r2, r3, gain_ref, keep_ref, send_ref, table_ref):
    core = at_ref[0]
    expert = at_ref[1].astype(jnp.float32)
    rows = (r0, r1, r2, r3)
    named = []
    scale = []
    for r in rows:
        ids = r[:, WIDTH:].astype(jnp.float32)
        named.append(jnp.sum((ids == expert).astype(jnp.float32), axis=1, keepdims=True))
        x = r[:, :WIDTH].astype(jnp.float32)
        scale.append(lax.rsqrt(jnp.sum(x * x, axis=1, keepdims=True) / WIDTH + 1e-06))
    named = jnp.concatenate(named, axis=0)
    scale = jnp.concatenate(scale, axis=0)
    count = 4 * ROWS
    row = lax.broadcasted_iota(jnp.int32, (count, count), 0)
    col = lax.broadcasted_iota(jnp.int32, (count, count), 1)
    earlier = ((col < row) & ((col // ROWS) == (row // ROWS))).astype(jnp.float32)
    named = jnp.broadcast_to(named, (count, 128))
    before = jnp.dot(earlier, named, preferred_element_type=jnp.float32)
    group = lax.broadcasted_iota(jnp.int32, (count, 128), 0) // ROWS
    lane = lax.broadcasted_iota(jnp.int32, (count, 128), 1)
    place = (group * CAP + core * (4 * CAP)).astype(jnp.float32) + before
    hit = (named > 0.5) & (before < CAP - 0.5) & (lane.astype(jnp.float32) == place)
    table = hit.astype(jnp.bfloat16)
    table_ref[...] = table
    wide = WIDTH // 4
    for part in range(4):
        cols = pl.ds(part * wide, wide)
        x = jnp.concatenate([r[:, cols].astype(jnp.float32) for r in rows], axis=0)
        normed = (x * scale * gain_ref[:, cols]).astype(jnp.bfloat16)
        slots = lax.dot_general(
            table, normed, (((0,), (0,)), ((), ())), preferred_element_type=jnp.float32
        )[:SLOTS].astype(jnp.bfloat16)
        inner = pl.ds((part % 2) * wide, wide)

        @pl.when(core == part // 2)
        def _():
            keep_ref[:, inner] = slots

        @pl.when(core != part // 2)
        def _():
            send_ref[:, inner] = slots


def pick(at, rows, gain):
    vmem = pl.BlockSpec(memory_space=pltpu.VMEM)
    return pl.pallas_call(
        pick_kernel,
        out_shape=(
            jax.ShapeDtypeStruct((SLOTS, HALF), jnp.bfloat16),
            jax.ShapeDtypeStruct((SLOTS, HALF), jnp.bfloat16),
            jax.ShapeDtypeStruct((4 * ROWS, 128), jnp.bfloat16),
        ),
        in_specs=[pl.BlockSpec(memory_space=pltpu.SMEM)] + [vmem] * 5,
        out_specs=(vmem, vmem, vmem),
        cost_estimate=pl.CostEstimate(
            flops=2 * 128 * 32 * WIDTH, bytes_accessed=2 * 72 * WIDTH, transcendentals=32
        ),
        compiler_params=pltpu.CompilerParams(vmem_limit_bytes=16 * 1024 * 1024),
    )(at, *rows, gain)


def attend(queries, latent_cache, cache_lengths):
    scores = (
        jnp.einsum("shk,slk->shl", queries, latent_cache, preferred_element_type=jnp.float32)
        * score_scale
    )
    visible = (
        jnp.arange(latent_cache.shape[1], dtype=jnp.int32)[None, None, :]
        < cache_lengths[:, None, None]
    )
    scores = jnp.where(visible, scores, jnp.float32(-1e30))
    peak = jnp.max(scores, axis=2, keepdims=True)
    powered = jnp.exp(scores - peak)
    probs = (powered / jnp.sum(powered, axis=2, keepdims=True)).astype(jnp.bfloat16)
    return jnp.einsum(
        "shl,slk->shk", probs, latent_cache[:, :, :LATENT], preferred_element_type=jnp.float32
    ).astype(jnp.bfloat16)


def local(
    queries,
    latent_cache,
    cache_lengths,
    stream,
    norm_gain,
    expert_ids,
    route_weights,
    w_gate,
    w_up,
    w_down,
):
    sec = lax.axis_index("sec")
    dev = lax.axis_index("dev")
    xl, core = sec // 2, sec % 2
    xh, z = dev // 32, (dev // 4) % 8
    expert = xh * 8 + z

    ids_wide = jnp.pad(expert_ids.astype(jnp.bfloat16), ((0, 0), (0, 120)), constant_values=-1)
    block = jnp.concatenate([stream, ids_wide], axis=1)
    arrived = {k: spread(block, k, 1) for k in ORDER}

    gate_halves = w_gate[0].reshape(2, HALF, 128)
    up_halves = w_up[0].reshape(2, HALF, 128)
    down_halves = w_down[0].reshape(128, 2, HALF)

    def half(array, which, axis):
        return lax.dynamic_index_in_dim(array, which, axis, keepdims=False)

    w_own = jnp.concatenate([half(gate_halves, core, 0), half(up_halves, core, 0)], axis=1)
    w_send = jnp.concatenate([half(gate_halves, 1 - core, 0), half(up_halves, 1 - core, 0)], axis=1)
    w_other = swap_core(w_send)
    down_own = half(down_halves, core, 1)
    down_other = swap_core(half(down_halves, 1 - core, 1))

    context = attend(queries, latent_cache, cache_lengths)

    at = jnp.stack([core, expert]).astype(jnp.int32)
    keep, give, table = pick(at, [arrived[k] for k in range(4)], norm_gain[None, :])
    mine = keep + swap_core(give)

    blocks = [mine] + [across(mine, dxl, dy) for dxl, dy in DELTAS]

    def experts(part):
        x = jnp.concatenate(part, axis=0)
        own = jnp.dot(x, w_own, preferred_element_type=jnp.float32)
        other = jnp.dot(x, w_other, preferred_element_type=jnp.float32)
        got = swap_core(jnp.concatenate([own, other], axis=1))
        own = own + got[:, 256:]
        other = other + got[:, :256]
        hidden = jnp.concatenate(
            [
                (jax.nn.silu(v[:, :128]) * v[:, 128:]).astype(jnp.bfloat16)
                for v in (own, other)
            ],
            axis=1,
        )
        down = jnp.concatenate([down_own, down_other], axis=0)
        out = jnp.dot(hidden, down, preferred_element_type=jnp.float32).astype(jnp.bfloat16)
        return [out[i * SLOTS : (i + 1) * SLOTS] for i in range(len(part))]

    sums = experts(blocks[:4]) + experts(blocks[4:])
    total = sums[0].astype(jnp.float32)
    for value, (dxl, dy) in zip(sums[1:], DELTAS):
        total = total + across(value, dxl, -dy).astype(jnp.float32)
    total = total.astype(jnp.bfloat16)
    whole = jnp.concatenate([total, swap_core(total)], axis=1)
    dense = jnp.dot(table[:, :SLOTS], whole, preferred_element_type=jnp.float32).astype(
        jnp.bfloat16
    )
    returned = {k: spread(dense[k * ROWS : (k + 1) * ROWS], k, -1) for k in ORDER}

    moe = jnp.zeros((ROWS, WIDTH), jnp.float32)
    for k in range(4):
        step = jnp.where(core == 0, k, -(k + 1))
        source = (xh ^ xl) * 8 + (z + step) % 8
        weight = jnp.sum(
            route_weights * (expert_ids == source).astype(jnp.float32), axis=1, keepdims=True
        )
        moe = moe + weight * returned[k].astype(jnp.float32)
    part = moe.astype(jnp.bfloat16)
    got = swap_core(part)
    swapped = jnp.concatenate([got[:, HALF:], got[:, :HALF]], axis=1)
    pair = part.astype(jnp.float32) + swapped.astype(jnp.float32)
    pair_sent = pair.astype(jnp.bfloat16)
    far = send(pair_sent, lambda xl, c, xh, z, y: (1 - xl, c, xh, z, y))
    full = pair_sent.astype(jnp.float32) + far.astype(jnp.float32)
    first, second = full[:, :HALF], full[:, HALF:]
    full = jnp.where(
        core == 0,
        jnp.concatenate([first, second], axis=1),
        jnp.concatenate([second, first], axis=1),
    )
    mixed = (stream.astype(jnp.float32) + full).astype(jnp.bfloat16)
    return (context, mixed)


def solution(mesh):
    return jax.shard_map(
        local,
        mesh=mesh,
        in_specs=(
            P(("sec", "dev"), None, None),
            P(("sec", "dev"), None, None),
            P(("sec", "dev")),
            P("dev", None),
            P(),
            P("dev", None),
            P("dev", None),
            P("dev", None, "sec"),
            P("dev", None, "sec"),
            P("dev", "sec", None),
        ),
        out_specs=(P(("sec", "dev"), None, None), P("dev", None)),
        check_vma=False,
    )
```

```python
import functools

import jax
import jax.numpy as jnp
from jax import lax
from jax.experimental import pallas as pl
from jax.experimental.pallas import tpu as pltpu
from jax.sharding import PartitionSpec as P

LATENT = 512
CAP = 5
ROWS = 8
WIDTH = 7168
SLOTS = 24
score_scale = 192.0 ** (-0.5)

SIZES = (2, 2, 2, 8, 4)


def pairs(move):
    out = []
    for xl in range(2):
        for c in range(2):
            for xh in range(2):
                for z in range(8):
                    for y in range(4):
                        place = (xl, c, xh, z, y)
                        lin = []
                        for spot in (place, move(*place)):
                            at = 0
                            for part, size in zip(spot, SIZES):
                                at = at * size + part % size
                            lin.append(at)
                        out.append(tuple(lin))
    return out


def send(value, move):
    return lax.ppermute(value, ("sec", "dev"), pairs(move))


def swap_core(value):
    return send(value, lambda xl, c, xh, z, y: (xl, 1 - c, xh, z, y))


STEPS = ((0, 1, -2, 3), (-1, 2, -3, 4))


def spread(value, k, sign):
    def move(xl, c, xh, z, y):
        if xl == c:
            return (xl, c, xh, z + sign * STEPS[c][k], y)
        return (1 - xl, 1 - c, 1 - xh, z + (STEPS[c][k] if sign > 0 else -STEPS[1 - c][k]), y)

    return send(value, move)


ORDER = (0, 1, 2, 3)


def pick_kernel(at_ref, r0, r1, r2, r3, gain_ref, slots_ref, table_ref):
    expert = at_ref[0].astype(jnp.float32)
    rows = (r0, r1, r2, r3)
    named = []
    scale = []
    for r in rows:
        ids = r[:, WIDTH:].astype(jnp.float32)
        named.append(jnp.sum((ids == expert).astype(jnp.float32), axis=1, keepdims=True))
        x = r[:, :WIDTH].astype(jnp.float32)
        scale.append(lax.rsqrt(jnp.sum(x * x, axis=1, keepdims=True) / WIDTH + 1e-06))
    named = jnp.concatenate(named, axis=0)
    scale = jnp.concatenate(scale, axis=0)
    count = 4 * ROWS
    row = lax.broadcasted_iota(jnp.int32, (count, count), 0)
    col = lax.broadcasted_iota(jnp.int32, (count, count), 1)
    earlier = ((col < row) & ((col // ROWS) == (row // ROWS))).astype(jnp.float32)
    named = jnp.broadcast_to(named, (count, 128))
    before = jnp.dot(earlier, named, preferred_element_type=jnp.float32)
    group = lax.broadcasted_iota(jnp.int32, (count, 128), 0) // ROWS
    lane = lax.broadcasted_iota(jnp.int32, (count, 128), 1)
    place = (group * CAP).astype(jnp.float32) + before
    hit = (named > 0.5) & (before < CAP - 0.5) & (lane.astype(jnp.float32) == place)
    table = hit.astype(jnp.bfloat16)
    table_ref[...] = table
    wide = WIDTH // 4
    for part in range(4):
        cols = pl.ds(part * wide, wide)
        x = jnp.concatenate([r[:, cols].astype(jnp.float32) for r in rows], axis=0)
        normed = (x * scale * gain_ref[:, cols]).astype(jnp.bfloat16)
        slots_ref[:, cols] = lax.dot_general(
            table, normed, (((0,), (0,)), ((), ())), preferred_element_type=jnp.float32
        )[:SLOTS].astype(jnp.bfloat16)


def pick(at, rows, gain):
    vmem = pl.BlockSpec(memory_space=pltpu.VMEM)
    return pl.pallas_call(
        pick_kernel,
        out_shape=(
            jax.ShapeDtypeStruct((SLOTS, WIDTH), jnp.bfloat16),
            jax.ShapeDtypeStruct((4 * ROWS, 128), jnp.bfloat16),
        ),
        in_specs=[pl.BlockSpec(memory_space=pltpu.SMEM)] + [vmem] * 5,
        out_specs=(vmem, vmem),
        cost_estimate=pl.CostEstimate(
            flops=2 * 128 * 32 * WIDTH, bytes_accessed=2 * 72 * WIDTH, transcendentals=32
        ),
        compiler_params=pltpu.CompilerParams(vmem_limit_bytes=16 * 1024 * 1024),
    )(at, *rows, gain)


def widen_kernel(stream_ref, ids_ref, out_ref):
    out_ref[:, :WIDTH] = stream_ref[...]
    out_ref[:, WIDTH:] = jnp.full((ROWS, 128), -1, jnp.bfloat16)
    out_ref[:, WIDTH : WIDTH + 8] = ids_ref[...].astype(jnp.float32).astype(jnp.bfloat16)


def widen(stream, ids):
    vmem = pl.BlockSpec(memory_space=pltpu.VMEM)
    return pl.pallas_call(
        widen_kernel,
        out_shape=jax.ShapeDtypeStruct((ROWS, WIDTH + 128), jnp.bfloat16),
        in_specs=[vmem, vmem],
        out_specs=vmem,
    )(stream, ids)


def expert_kernel(count, *refs):
    blocks = refs[:count]
    gates = refs[count : count + 2]
    ups = refs[count + 2 : count + 4]
    downs = refs[count + 4 : count + 6]
    outs = refs[count + 6 :]
    step = 1024
    acc = jnp.zeros((count * SLOTS, 512), jnp.float32)
    for at in range(0, WIDTH, step):
        ks = pl.ds(at, step)
        x = jnp.concatenate([b[:, ks].astype(jnp.float32) for b in blocks], axis=0)
        w = jnp.concatenate([r[ks, :] for r in gates + ups], axis=1)
        acc = acc + jnp.dot(x.astype(jnp.bfloat16), w, preferred_element_type=jnp.float32)
    gate_proj, up_proj = acc[:, :256], acc[:, 256:]
    hidden = (gate_proj / (1.0 + jnp.exp(-gate_proj)) * up_proj).astype(jnp.bfloat16)
    for at in range(0, WIDTH, step):
        ks = pl.ds(at, step)
        w = jnp.concatenate([r[:, ks] for r in downs], axis=0)
        out = jnp.dot(hidden, w, preferred_element_type=jnp.float32)
        for i, ref in enumerate(outs):
            ref[:, ks] = out[i * SLOTS : (i + 1) * SLOTS].astype(jnp.bfloat16)


def experts(blocks, gates, ups, downs):
    vmem = pl.BlockSpec(memory_space=pltpu.VMEM)
    count = len(blocks)
    rows = count * SLOTS
    return pl.pallas_call(
        functools.partial(expert_kernel, count),
        out_shape=tuple(jax.ShapeDtypeStruct((SLOTS, WIDTH), jnp.bfloat16) for _ in blocks),
        in_specs=[vmem] * (count + 6),
        out_specs=tuple(vmem for _ in blocks),
        cost_estimate=pl.CostEstimate(
            flops=2 * rows * WIDTH * 768,
            bytes_accessed=2 * WIDTH * (768 + 2 * rows),
            transcendentals=rows * 256,
        ),
        compiler_params=pltpu.CompilerParams(vmem_limit_bytes=32 * 1024 * 1024),
    )(*blocks, *gates, *ups, *downs)


def scatter_kernel(table_ref, b0, b1, b2, b3, o0, o1, o2, o3):
    table = table_ref[...][:, :SLOTS]
    wide = WIDTH // 4
    for part in range(4):
        cols = pl.ds(part * wide, wide)
        total = b0[:, cols].astype(jnp.float32)
        for b in (b1, b2, b3):
            total = total + b[:, cols].astype(jnp.float32)
        dense = jnp.dot(table, total.astype(jnp.bfloat16), preferred_element_type=jnp.float32)
        for i, out in enumerate((o0, o1, o2, o3)):
            out[:, cols] = dense[i * ROWS : (i + 1) * ROWS].astype(jnp.bfloat16)


def scatter(table, blocks):
    vmem = pl.BlockSpec(memory_space=pltpu.VMEM)
    return pl.pallas_call(
        scatter_kernel,
        out_shape=tuple(jax.ShapeDtypeStruct((ROWS, WIDTH), jnp.bfloat16) for _ in range(4)),
        in_specs=[vmem] * 5,
        out_specs=(vmem,) * 4,
        cost_estimate=pl.CostEstimate(
            flops=2 * 32 * 32 * WIDTH, bytes_accessed=2 * 152 * WIDTH, transcendentals=0
        ),
        compiler_params=pltpu.CompilerParams(vmem_limit_bytes=16 * 1024 * 1024),
    )(table, *blocks)


def attend_kernel(length_ref, q_hbm, cache_hbm, out_ref, q_ref, cache_ref, sems):
    parts, _, size = cache_ref.shape
    heads = q_ref.shape[1]
    copies = [pltpu.make_async_copy(q_hbm.at[0], q_ref, sems.at[parts])]
    for part in range(parts):
        copies.append(
            pltpu.make_async_copy(
                cache_hbm.at[0, :, pl.ds(part * size, size)], cache_ref.at[part], sems.at[part]
            )
        )
    for copy in copies:
        copy.start()
    copies[0].wait()
    peak = jnp.full((heads, 1), -1e30, jnp.float32)
    total = jnp.zeros((heads, 1), jnp.float32)
    acc = jnp.zeros((heads, LATENT), jnp.float32)
    query = q_ref[...]
    for part in range(parts):
        copies[part + 1].wait()
        scores = (
            lax.dot_general(
                query,
                cache_ref[part],
                (((0,), (0,)), ((), ())),
                preferred_element_type=jnp.float32,
            )
            * score_scale
        )
        at = part * size + lax.broadcasted_iota(jnp.int32, scores.shape, 1)
        scores = jnp.where(at < length_ref[0], scores, jnp.float32(-1e30))
        new = jnp.maximum(peak, jnp.max(scores, axis=1, keepdims=True))
        powered = jnp.exp(scores - new)
        fade = jnp.exp(peak - new)
        total = total * fade + jnp.sum(powered, axis=1, keepdims=True)
        peak = new
        acc = acc * fade + lax.dot_general(
            powered.astype(jnp.bfloat16),
            cache_ref[part, :LATENT],
            (((1,), (1,)), ((), ())),
            preferred_element_type=jnp.float32,
        )
    out_ref[0] = (acc / total).astype(jnp.bfloat16)


def attend(queries, latent_cache, cache_lengths):
    heads, width = queries.shape[1:]
    length = latent_cache.shape[1]
    parts = 4
    return pl.pallas_call(
        attend_kernel,
        out_shape=jax.ShapeDtypeStruct((1, heads, LATENT), jnp.bfloat16),
        in_specs=[
            pl.BlockSpec(memory_space=pltpu.SMEM),
            pl.BlockSpec(memory_space=pltpu.HBM),
            pl.BlockSpec(memory_space=pltpu.HBM),
        ],
        out_specs=pl.BlockSpec(memory_space=pltpu.VMEM),
        scratch_shapes=[
            pltpu.VMEM((width, heads), jnp.bfloat16),
            pltpu.VMEM((parts, width, length // parts), jnp.bfloat16),
            pltpu.SemaphoreType.DMA((parts + 1,)),
        ],
        cost_estimate=pl.CostEstimate(
            flops=2 * heads * length * (width + LATENT),
            bytes_accessed=2 * length * width,
            transcendentals=heads * length,
        ),
        compiler_params=pltpu.CompilerParams(vmem_limit_bytes=16 * 1024 * 1024),
    )(cache_lengths, jnp.swapaxes(queries, 1, 2), jnp.swapaxes(latent_cache, 1, 2))


def local(
    queries,
    latent_cache,
    cache_lengths,
    stream,
    norm_gain,
    expert_ids,
    route_weights,
    w_gate,
    w_up,
    w_down,
):
    sec = lax.axis_index("sec")
    dev = lax.axis_index("dev")
    xl, core = sec // 2, sec % 2
    xh, z = dev // 32, (dev // 4) % 8
    expert = xh * 8 + z

    block = widen(stream, expert_ids)
    arrived = {k: spread(block, k, 1) for k in ORDER}

    gate_own, up_own, down_own = w_gate[0], w_up[0], w_down[0]
    block, gate_own = lax.optimization_barrier((block, gate_own))
    gate_other = swap_core(gate_own)
    context = attend(queries, latent_cache, cache_lengths)
    rows = [arrived[k] for k in range(4)]
    rows[1], context = lax.optimization_barrier((rows[1], context))
    at = expert.astype(jnp.int32)[None]
    mine, table = pick(at, rows, norm_gain[None, :])

    def over(value):
        return send(value, lambda xl, c, xh, z, y: (1 - xl, c, xh, z, y))

    def along(value, sign, flip=0):
        return send(
            value,
            lambda xl, c, xh, z, y: (xl ^ flip, c, xh, z, y + (sign if c == 0 else -sign)),
        )

    mine, up_own, gate_other = lax.optimization_barrier((mine, up_own, gate_other))
    up_other = swap_core(up_own)
    x_in = over(mine)
    p_in = along(mine, 1)
    m_in = along(mine, -1)
    x_in, p_in, m_in, up_other, down_own = lax.optimization_barrier(
        (x_in, p_in, m_in, up_other, down_own)
    )
    down_other = swap_core(down_own)
    weights = ((gate_own, gate_other), (up_own, up_other), (down_own, down_other))
    pxp_in = along(p_in, 1, 1)
    pp_in = along(p_in, 1)
    xp_in = along(x_in, 1)
    mx_in = over(m_in)
    own, x_out, p_out, m_out = experts([mine, x_in, p_in, m_in], *weights)
    pxp_in, own = lax.optimization_barrier((pxp_in, own))
    pxp_out, pp_out, xp_out, mx_out = experts([pxp_in, pp_in, xp_in, mx_in], *weights)
    pxp_back = along(pxp_out, -1, 1)
    pp_back = along(pp_out, -1)
    xp_back = along(xp_out, -1)
    mx_back = over(mx_out)

    def add(*values):
        return sum(v.astype(jnp.float32) for v in values).astype(jnp.bfloat16)

    p_back = along(add(p_out, pp_back, pxp_back), -1)
    m_back = along(add(m_out, mx_back), 1)
    x_back = over(add(x_out, xp_back))
    dense = scatter(table, (own, p_back, m_back, x_back))
    returned = {k: spread(dense[k], k, -1) for k in ORDER}

    moe = jnp.zeros((ROWS, WIDTH), jnp.float32)
    for k in range(4):
        step = jnp.where(core == 0, STEPS[0][k], STEPS[1][k])
        source = jnp.where(xl == core, xh, 1 - xh) * 8 + (z + step) % 8
        weight = jnp.sum(
            route_weights * (expert_ids == source).astype(jnp.float32), axis=1, keepdims=True
        )
        moe = moe + weight * returned[k].astype(jnp.float32)
    part = moe.astype(jnp.bfloat16)
    pair = part.astype(jnp.float32) + swap_core(part).astype(jnp.float32)
    pair = pair.astype(jnp.bfloat16)
    far = over(pair)
    full = pair.astype(jnp.float32) + far.astype(jnp.float32)
    mixed = (stream.astype(jnp.float32) + full).astype(jnp.bfloat16)
    return (context, mixed)


def solution(mesh):
    return jax.shard_map(
        local,
        mesh=mesh,
        in_specs=(
            P(("sec", "dev"), None, None),
            P(("sec", "dev"), None, None),
            P(("sec", "dev")),
            P("dev", None),
            P(),
            P("dev", None),
            P("dev", None),
            P("dev", None, "sec"),
            P("dev", None, "sec"),
            P("dev", "sec", None),
        ),
        out_specs=(P(("sec", "dev"), None, None), P("dev", None)),
        check_vma=False,
    )
```

```python
import functools

import jax
import jax.numpy as jnp
from jax import lax
from jax.experimental import pallas as pl
from jax.experimental.pallas import tpu as pltpu
from jax.sharding import PartitionSpec as P

LATENT = 512
CAP = 5
ROWS = 8
WIDTH = 7168
PIECES = 8
PIECE = 896
score_scale = 192.0 ** (-0.5)

SIZES = (2, 2, 2, 8, 4)


def pairs(move):
    out = []
    for xl in range(2):
        for c in range(2):
            for xh in range(2):
                for z in range(8):
                    for y in range(4):
                        place = (xl, c, xh, z, y)
                        lin = []
                        for spot in (place, move(*place)):
                            at = 0
                            for part, size in zip(spot, SIZES):
                                at = at * size + part % size
                            lin.append(at)
                        out.append(tuple(lin))
    return out


def send(value, move):
    return lax.ppermute(value, ("sec", "dev"), pairs(move))


def swap_core(value):
    return send(value, lambda xl, c, xh, z, y: (xl, 1 - c, xh, z, y))


STEPS = ((0, 1, -2, 3), (-1, 2, -3, 4))


def spread(value, k, sign):
    def move(xl, c, xh, z, y):
        if xl == c:
            return (xl, c, xh, z + sign * STEPS[c][k], y)
        return (1 - xl, 1 - c, 1 - xh, z + (STEPS[c][k] if sign > 0 else -STEPS[1 - c][k]), y)

    return send(value, move)


ORDER = (0, 1, 2, 3)


VMEM = pl.BlockSpec(memory_space=pltpu.VMEM)
PACKED = jax.ShapeDtypeStruct((CAP * PIECES, PIECE), jnp.bfloat16)
BLOCK = jax.ShapeDtypeStruct((4 * CAP * PIECES, PIECE), jnp.bfloat16)


def limit(mib):
    return pltpu.CompilerParams(vmem_limit_bytes=mib * 1024 * 1024)


def pack_kernel(at_ref, *refs):
    sources, (o0, o1, o2, o3, table_ref) = refs[:4], refs[4:9]
    scratch, sems = refs[9:13], refs[13]
    copies = [
        pltpu.make_async_copy(a, b, sems.at[i]) for i, (a, b) in enumerate(zip(sources, scratch))
    ]
    for copy in copies:
        copy.start()
    for copy in copies:
        copy.wait()
    stream_ref, gain_ref, ids_ref, route_ref = scratch
    lane = lax.broadcasted_iota(jnp.int32, (ROWS, 256), 1)
    target, slot, piece = lane // (CAP * PIECES), (lane // PIECES) % CAP, lane % PIECES
    wanted = jnp.full((ROWS, 256), -1, jnp.int32)
    for k in range(4):
        wanted = jnp.where(target == k, at_ref[k], wanted)
    named = jnp.zeros((ROWS, 256), jnp.float32)
    weight = jnp.zeros((ROWS, 256), jnp.float32)
    ids, route = ids_ref[...], route_ref[...]
    for t in range(ids.shape[1]):
        same = (ids[:, t : t + 1] == wanted).astype(jnp.float32)
        named = named + same
        weight = weight + same * route[:, t : t + 1]
    row = lax.broadcasted_iota(jnp.int32, (ROWS, ROWS), 0)
    col = lax.broadcasted_iota(jnp.int32, (ROWS, ROWS), 1)
    before = jnp.dot((col < row).astype(jnp.float32), named, preferred_element_type=jnp.float32)
    hit = jnp.where(jnp.abs(before - slot.astype(jnp.float32)) < 0.5, named, 0.0)
    table_ref[...] = hit * weight
    picked = jnp.concatenate([jnp.where(piece == p, hit, 0.0) for p in range(PIECES)], axis=0)
    x = stream_ref[...].astype(jnp.float32)
    scale = lax.rsqrt(jnp.sum(x * x, axis=1, keepdims=True) / WIDTH + 1e-06)
    normed = x * scale * gain_ref[...]
    normed = jnp.concatenate(
        [normed[:, p * PIECE : (p + 1) * PIECE] for p in range(PIECES)], axis=0
    )
    out = lax.dot_general(
        picked.astype(jnp.bfloat16),
        normed.astype(jnp.bfloat16),
        (((0,), (0,)), ((), ())),
        preferred_element_type=jnp.float32,
    )
    for k, ref in enumerate((o0, o1, o2, o3)):
        ref[...] = out[k * CAP * PIECES : (k + 1) * CAP * PIECES].astype(jnp.bfloat16)


def pack(at, stream, gain, ids, route):
    return pl.pallas_call(
        pack_kernel,
        out_shape=(PACKED,) * 4 + (jax.ShapeDtypeStruct((ROWS, 256), jnp.float32),),
        in_specs=[pl.BlockSpec(memory_space=pltpu.SMEM)] + [pl.BlockSpec(memory_space=pl.ANY)] * 4,
        out_specs=(VMEM,) * 5,
        scratch_shapes=[pltpu.VMEM(v.shape, v.dtype) for v in (stream, gain, ids, route)]
        + [pltpu.SemaphoreType.DMA((4,))],
        compiler_params=limit(60),
    )(at, stream, gain, ids, route)


def join_kernel(a, b, c, d, out):
    rows = [ref[...].astype(jnp.float32) for ref in (a, b, c, d)]
    out[...] = jnp.concatenate(rows, axis=0).astype(jnp.bfloat16)


def join(parts):
    return pl.pallas_call(
        join_kernel, out_shape=BLOCK, in_specs=[VMEM] * 4, out_specs=VMEM, compiler_params=limit(8)
    )(*parts)


def split_kernel(b0, b1, b2, b3, b4, o0, o1, o2, o3):
    total = b0[...].astype(jnp.float32)
    for ref in (b1, b2, b3, b4):
        total = total + ref[...].astype(jnp.float32)
    for k, ref in enumerate((o0, o1, o2, o3)):
        ref[...] = total[k * CAP * PIECES : (k + 1) * CAP * PIECES].astype(jnp.bfloat16)


def split(blocks):
    return pl.pallas_call(
        split_kernel,
        out_shape=(PACKED,) * 4,
        in_specs=[VMEM] * 5,
        out_specs=(VMEM,) * 4,
        compiler_params=limit(8),
    )(*blocks)


def weigh_kernel(table_ref, a, b, c, d, out):
    rows = [ref[...].astype(jnp.float32) for ref in (a, b, c, d)]
    rows.append(jnp.zeros((256 - 4 * CAP * PIECES, PIECE), jnp.float32))
    rows = jnp.concatenate(rows, axis=0).astype(jnp.bfloat16)
    left = table_ref[...]
    parts = []
    for _ in range(3):
        part = left.astype(jnp.bfloat16).astype(jnp.float32)
        parts.append(part)
        left = left - part
    parts = jnp.concatenate(parts, axis=0)
    piece = lax.broadcasted_iota(jnp.int32, parts.shape, 1) % PIECES
    lhs = jnp.concatenate([jnp.where(piece == p, parts, 0.0) for p in range(PIECES)], axis=0)
    sums = jnp.dot(lhs.astype(jnp.bfloat16), rows, preferred_element_type=jnp.float32)
    for p in range(PIECES):
        at = p * 3 * ROWS
        total = sums[at : at + ROWS]
        total = total + sums[at + ROWS : at + 2 * ROWS] + sums[at + 2 * ROWS : at + 3 * ROWS]
        out[:, p * PIECE : (p + 1) * PIECE] = total.astype(jnp.bfloat16)


def weigh(table, parts):
    return pl.pallas_call(
        weigh_kernel,
        out_shape=jax.ShapeDtypeStruct((ROWS, WIDTH), jnp.bfloat16),
        in_specs=[VMEM] * 5,
        out_specs=VMEM,
        compiler_params=limit(8),
    )(table, *parts)


def expert_kernel(count, rows, *refs):
    blocks = refs[:count]
    wide = refs[count : count + 3]
    down = refs[count + 3]
    outs = refs[count + 4 : -1]
    work = refs[-1]
    size = 4 * CAP * PIECES
    lanes = work.shape[0]
    for i, ref in enumerate(blocks):
        block = ref[...].astype(jnp.float32)
        for t in range(lanes):
            work[t, i * size : (i + 1) * size] = block[:, t * 128 : (t + 1) * 128]
    rest = rows * PIECES - count * size
    for t in range(lanes):
        work[t, count * size :] = jnp.zeros((rest, 128), jnp.float32)
    acc = jnp.zeros((rows, 512), jnp.float32)
    for p in range(PIECES):
        ks = pl.ds(p * PIECE, PIECE)
        x = jnp.concatenate(
            [work[t, pl.ds(p, rows, stride=PIECES), :] for t in range(lanes)], axis=1
        ).astype(jnp.bfloat16)
        w = jnp.concatenate([r[ks, :] for r in wide], axis=1)
        acc = acc + jnp.dot(x, w, preferred_element_type=jnp.float32)
    gate_proj = jnp.concatenate([acc[:, :128], acc[:, 256:384]], axis=1)
    up_proj = jnp.concatenate([acc[:, 128:256], acc[:, 384:]], axis=1)
    hidden = (gate_proj / (1.0 + jnp.exp(-gate_proj)) * up_proj).astype(jnp.bfloat16)
    for p in range(PIECES):
        ks = pl.ds(p * PIECE, PIECE)
        out = jnp.dot(hidden, down[:, ks], preferred_element_type=jnp.float32)
        for t in range(lanes):
            work[t, pl.ds(p, rows, stride=PIECES), :] = out[:, t * 128 : (t + 1) * 128]
    for i, ref in enumerate(outs):
        for t in range(lanes):
            part = work[t, i * size : (i + 1) * size]
            ref[:, t * 128 : (t + 1) * 128] = part.astype(jnp.bfloat16)


def experts(blocks, *weights):
    count = len(blocks)
    rows = -(-count * 4 * CAP // 16) * 16
    return pl.pallas_call(
        functools.partial(expert_kernel, count, rows),
        out_shape=(BLOCK,) * count,
        in_specs=[VMEM] * (count + 4),
        out_specs=(VMEM,) * count,
        scratch_shapes=[pltpu.VMEM((PIECE // 128, rows * PIECES, 128), jnp.float32)],
        cost_estimate=pl.CostEstimate(
            flops=2 * rows * WIDTH * 768,
            bytes_accessed=2 * WIDTH * (768 + 2 * rows),
            transcendentals=rows * 256,
        ),
        compiler_params=limit(32),
    )(*blocks, *weights)


def attend_kernel(length_ref, q_hbm, cache_hbm, out_ref, q_ref, cache_ref, sems):
    parts, _, size = cache_ref.shape
    heads = q_ref.shape[1]
    copies = [pltpu.make_async_copy(q_hbm.at[0], q_ref, sems.at[parts])]
    for part in range(parts):
        copies.append(
            pltpu.make_async_copy(
                cache_hbm.at[0, :, pl.ds(part * size, size)], cache_ref.at[part], sems.at[part]
            )
        )
    for copy in copies:
        copy.start()
    copies[0].wait()
    peak = jnp.full((heads, 1), -1e30, jnp.float32)
    total = jnp.zeros((heads, 1), jnp.float32)
    acc = jnp.zeros((heads, LATENT), jnp.float32)
    query = q_ref[...]
    for part in range(parts):
        copies[part + 1].wait()
        scores = (
            lax.dot_general(
                query,
                cache_ref[part],
                (((0,), (0,)), ((), ())),
                preferred_element_type=jnp.float32,
            )
            * score_scale
        )
        at = part * size + lax.broadcasted_iota(jnp.int32, scores.shape, 1)
        scores = jnp.where(at < length_ref[0], scores, jnp.float32(-1e30))
        new = jnp.maximum(peak, jnp.max(scores, axis=1, keepdims=True))
        powered = jnp.exp(scores - new)
        fade = jnp.exp(peak - new)
        total = total * fade + jnp.sum(powered, axis=1, keepdims=True)
        peak = new
        acc = acc * fade + lax.dot_general(
            powered.astype(jnp.bfloat16),
            cache_ref[part, :LATENT],
            (((1,), (1,)), ((), ())),
            preferred_element_type=jnp.float32,
        )
    out_ref[0] = (acc / total).astype(jnp.bfloat16)


def attend(queries, latent_cache, cache_lengths):
    heads, width = queries.shape[1:]
    length = latent_cache.shape[1]
    parts = 4
    return pl.pallas_call(
        attend_kernel,
        out_shape=jax.ShapeDtypeStruct((1, heads, LATENT), jnp.bfloat16),
        in_specs=[
            pl.BlockSpec(memory_space=pltpu.SMEM),
            pl.BlockSpec(memory_space=pltpu.HBM),
            pl.BlockSpec(memory_space=pltpu.HBM),
        ],
        out_specs=pl.BlockSpec(memory_space=pltpu.VMEM),
        scratch_shapes=[
            pltpu.VMEM((width, heads), jnp.bfloat16),
            pltpu.VMEM((parts, width, length // parts), jnp.bfloat16),
            pltpu.SemaphoreType.DMA((parts + 1,)),
        ],
        cost_estimate=pl.CostEstimate(
            flops=2 * heads * length * (width + LATENT),
            bytes_accessed=2 * length * width,
            transcendentals=heads * length,
        ),
        compiler_params=limit(60),
    )(cache_lengths, jnp.swapaxes(queries, 1, 2), jnp.swapaxes(latent_cache, 1, 2))


def local(
    queries,
    latent_cache,
    cache_lengths,
    stream,
    norm_gain,
    expert_ids,
    route_weights,
    w_gate,
    w_up,
    w_down,
):
    sec = lax.axis_index("sec")
    dev = lax.axis_index("dev")
    xl, core = sec // 2, sec % 2
    xh, z = dev // 32, (dev // 4) % 8

    half = jnp.where(xl == core, xh, 1 - xh) * 8
    at = [half + (z + jnp.where(core == 0, STEPS[0][k], STEPS[1][k])) % 8 for k in range(4)]
    at = jnp.stack(at).astype(jnp.int32)
    *packed, table = pack(at, stream, norm_gain[None, :], expert_ids, route_weights)
    gate_own, up_own, down_own = w_gate[0], w_up[0], w_down[0]
    gate_other = swap_core(gate_own)
    packed[1], up_own, gate_other = lax.optimization_barrier((packed[1], up_own, gate_other))
    arrived = [spread(packed[k], k, 1) for k in range(4)]

    up_other = swap_core(up_own)
    wide_own = jnp.concatenate([gate_own, up_own], axis=1)
    mine = join(arrived)

    def over(value):
        return send(value, lambda xl, c, xh, z, y: (1 - xl, c, xh, z, y))

    def along(value, dy):
        return send(value, lambda xl, c, xh, z, y: (xl, c, xh, z, y + dy))

    mine, down_own, up_other, wide_own = lax.optimization_barrier(
        (mine, down_own, up_other, wide_own)
    )
    down_other = swap_core(down_own)
    x_in = over(mine)
    up_in = along(mine, 1)
    dn_in = along(mine, -1)
    y2_in = along(mine, 2)
    x_in, y2_in, down_other = lax.optimization_barrier((x_in, y2_in, down_other))
    down = jnp.concatenate([down_own, down_other], axis=0)
    weights = (wide_own, gate_other, up_other, down)
    x_up_in = along(x_in, 1)
    x_dn_in = along(x_in, -1)
    x_y2_in = over(y2_in)
    own, x_out, y2_out, up_out, dn_out = experts([mine, x_in, y2_in, up_in, dn_in], *weights)
    x_up_in, own = lax.optimization_barrier((x_up_in, own))
    x_up_out, x_dn_out, x_y2_out = experts([x_up_in, x_dn_in, x_y2_in], *weights)
    up_back = along(up_out, -1)
    dn_back = along(dn_out, 1)
    x_up_back = along(x_up_out, -1)
    x_dn_back = along(x_dn_out, 1)
    x_y2_back = over(x_y2_out)

    def add(*values):
        return sum(v.astype(jnp.float32) for v in values).astype(jnp.bfloat16)

    x_sum = add(x_out, x_up_back, x_dn_back)
    y2_sum = add(y2_out, x_y2_back)
    x_sum, y2_sum, queries = lax.optimization_barrier((x_sum, y2_sum, queries))
    x_back = over(x_sum)
    y2_back = along(y2_sum, 2)
    context = attend(queries, latent_cache, cache_lengths)
    up_back, context = lax.optimization_barrier((up_back, context))
    back = split((own, up_back, dn_back, y2_back, x_back))
    returned = [spread(back[k], k, -1) for k in range(4)]
    part = weigh(table, returned)
    pair = part.astype(jnp.float32) + swap_core(part).astype(jnp.float32)
    pair = pair.astype(jnp.bfloat16)
    far = over(pair)
    full = pair.astype(jnp.float32) + far.astype(jnp.float32)
    mixed = (stream.astype(jnp.float32) + full).astype(jnp.bfloat16)
    return (context, mixed)


def solution(mesh):
    return jax.shard_map(
        local,
        mesh=mesh,
        in_specs=(
            P(("sec", "dev"), None, None),
            P(("sec", "dev"), None, None),
            P(("sec", "dev")),
            P("dev", None),
            P(),
            P("dev", None),
            P("dev", None),
            P("dev", None, "sec"),
            P("dev", None, "sec"),
            P("dev", "sec", None),
        ),
        out_specs=(P(("sec", "dev"), None, None), P("dev", None)),
        check_vma=False,
    )
```

```python
import functools

import jax
import jax.numpy as jnp
from jax import lax
from jax.experimental import pallas as pl
from jax.experimental.pallas import tpu as pltpu
from jax.sharding import PartitionSpec as P

LATENT = 512
CAP = 5
ROWS = 8
WIDTH = 7168
PIECES = 8
PIECE = 896
score_scale = 192.0 ** (-0.5)

SIZES = (2, 2, 2, 8, 4)


def pairs(move):
    out = []
    for xl in range(2):
        for c in range(2):
            for xh in range(2):
                for z in range(8):
                    for y in range(4):
                        place = (xl, c, xh, z, y)
                        lin = []
                        for spot in (place, move(*place)):
                            at = 0
                            for part, size in zip(spot, SIZES):
                                at = at * size + part % size
                            lin.append(at)
                        out.append(tuple(lin))
    return out


def send(value, move):
    return lax.ppermute(value, ("sec", "dev"), pairs(move))


def swap_core(value):
    return send(value, lambda xl, c, xh, z, y: (xl, 1 - c, xh, z, y))


STEPS = ((3, -2, 1, 0), (4, -3, 2, -1))


def spread(value, k, sign):
    def move(xl, c, xh, z, y):
        if xl == c:
            return (xl, c, xh, z + sign * STEPS[c][k], y)
        return (1 - xl, 1 - c, 1 - xh, z + (STEPS[c][k] if sign > 0 else -STEPS[1 - c][k]), y)

    return send(value, move)


ORDER = (0, 1, 2, 3)


VMEM = pl.BlockSpec(memory_space=pltpu.VMEM)
PACKED = jax.ShapeDtypeStruct((CAP * PIECES, PIECE), jnp.bfloat16)
BLOCK = jax.ShapeDtypeStruct((4 * CAP * PIECES, PIECE), jnp.bfloat16)


def limit(mib):
    return pltpu.CompilerParams(vmem_limit_bytes=mib * 1024 * 1024)


def targets():
    sec, dev = lax.axis_index("sec"), lax.axis_index("dev")
    xl, core = sec // 2, sec % 2
    xh, z = dev // 32, (dev // 4) % 8
    half = jnp.where(xl == core, xh, 1 - xh) * 8
    steps = [jnp.where(core == 0, STEPS[0][k], STEPS[1][k]) for k in range(4)]
    return [half + (z + step + 8) % 8 for step in steps]


def pack_kernel(*refs):
    sources, (o0, o1, o2, o3, table_ref) = refs[:4], refs[4:9]
    scratch, sems = refs[9:13], refs[13]
    copies = [
        pltpu.make_async_copy(a, b, sems.at[i]) for i, (a, b) in enumerate(zip(sources, scratch))
    ]
    for copy in copies:
        copy.start()
    for copy in copies:
        copy.wait()
    stream_ref, gain_ref, ids_ref, route_ref = scratch
    lane = lax.broadcasted_iota(jnp.int32, (ROWS, 256), 1)
    target, slot, piece = lane // (CAP * PIECES), (lane // PIECES) % CAP, lane % PIECES
    wanted = jnp.full((ROWS, 256), -1, jnp.int32)
    for k, expert in enumerate(targets()):
        wanted = jnp.where(target == k, expert, wanted)
    named = jnp.zeros((ROWS, 256), jnp.float32)
    weight = jnp.zeros((ROWS, 256), jnp.float32)
    ids, route = ids_ref[...], route_ref[...]
    for t in range(ids.shape[1]):
        same = (ids[:, t : t + 1] == wanted).astype(jnp.float32)
        named = named + same
        weight = weight + same * route[:, t : t + 1]
    row = lax.broadcasted_iota(jnp.int32, (ROWS, ROWS), 0)
    col = lax.broadcasted_iota(jnp.int32, (ROWS, ROWS), 1)
    before = jnp.dot((col < row).astype(jnp.float32), named, preferred_element_type=jnp.float32)
    hit = jnp.where(jnp.abs(before - slot.astype(jnp.float32)) < 0.5, named, 0.0)
    table_ref[...] = hit * weight
    picked = jnp.concatenate([jnp.where(piece == p, hit, 0.0) for p in range(PIECES)], axis=0)
    x = stream_ref[...].astype(jnp.float32)
    scale = lax.rsqrt(jnp.sum(x * x, axis=1, keepdims=True) / WIDTH + 1e-06)
    normed = x * scale * gain_ref[...]
    normed = jnp.concatenate(
        [normed[:, p * PIECE : (p + 1) * PIECE] for p in range(PIECES)], axis=0
    )
    out = lax.dot_general(
        picked.astype(jnp.bfloat16),
        normed.astype(jnp.bfloat16),
        (((0,), (0,)), ((), ())),
        preferred_element_type=jnp.float32,
    )
    for k, ref in enumerate((o0, o1, o2, o3)):
        ref[...] = out[k * CAP * PIECES : (k + 1) * CAP * PIECES].astype(jnp.bfloat16)


def pack(stream, gain, ids, route):
    return pl.pallas_call(
        pack_kernel,
        out_shape=(PACKED,) * 4 + (jax.ShapeDtypeStruct((ROWS, 256), jnp.float32),),
        in_specs=[pl.BlockSpec(memory_space=pl.ANY)] * 4,
        out_specs=(VMEM,) * 5,
        scratch_shapes=[pltpu.VMEM(v.shape, v.dtype) for v in (stream, gain, ids, route)]
        + [pltpu.SemaphoreType.DMA((4,))],
        compiler_params=limit(60),
    )(stream, gain, ids, route)


def join_kernel(a, b, c, d, out):
    rows = [ref[...].astype(jnp.float32) for ref in (a, b, c, d)]
    out[...] = jnp.concatenate(rows, axis=0).astype(jnp.bfloat16)


def join(parts):
    return pl.pallas_call(
        join_kernel, out_shape=BLOCK, in_specs=[VMEM] * 4, out_specs=VMEM, compiler_params=limit(8)
    )(*parts)


def split_kernel(b0, b1, b2, o0, o1, o2, o3):
    total = b0[...]
    for ref in (b1, b2):
        total = total + ref[...].astype(jnp.float32)
    for k, ref in enumerate((o0, o1, o2, o3)):
        ref[...] = total[k * CAP * PIECES : (k + 1) * CAP * PIECES].astype(jnp.bfloat16)


def split(blocks):
    return pl.pallas_call(
        split_kernel,
        out_shape=(PACKED,) * 4,
        in_specs=[VMEM] * 3,
        out_specs=(VMEM,) * 4,
        compiler_params=limit(8),
    )(*blocks)


def weigh_kernel(table_ref, a, b, c, d, out):
    rows = [ref[...].astype(jnp.float32) for ref in (a, b, c, d)]
    rows.append(jnp.zeros((256 - 4 * CAP * PIECES, PIECE), jnp.float32))
    rows = jnp.concatenate(rows, axis=0).astype(jnp.bfloat16)
    left = table_ref[...]
    parts = []
    for _ in range(3):
        part = left.astype(jnp.bfloat16).astype(jnp.float32)
        parts.append(part)
        left = left - part
    parts = jnp.concatenate(parts, axis=0)
    piece = lax.broadcasted_iota(jnp.int32, parts.shape, 1) % PIECES
    lhs = jnp.concatenate([jnp.where(piece == p, parts, 0.0) for p in range(PIECES)], axis=0)
    sums = jnp.dot(lhs.astype(jnp.bfloat16), rows, preferred_element_type=jnp.float32)
    for p in range(PIECES):
        at = p * 3 * ROWS
        total = sums[at : at + ROWS]
        total = total + sums[at + ROWS : at + 2 * ROWS] + sums[at + 2 * ROWS : at + 3 * ROWS]
        out[:, p * PIECE : (p + 1) * PIECE] = total.astype(jnp.bfloat16)


def weigh(table, parts):
    return pl.pallas_call(
        weigh_kernel,
        out_shape=jax.ShapeDtypeStruct((ROWS, WIDTH), jnp.bfloat16),
        in_specs=[VMEM] * 5,
        out_specs=VMEM,
        compiler_params=limit(8),
    )(table, *parts)


def expert_kernel(count, rows, *refs):
    blocks = refs[:count]
    wide = refs[count : count + 2]
    down = refs[count + 2]
    outs = refs[count + 3 : -1]
    work = refs[-1]
    size = 4 * CAP * PIECES
    lanes = work.shape[0]
    for i, ref in enumerate(blocks):
        block = ref[...].astype(jnp.float32)
        for t in range(lanes):
            work[t, i * size : (i + 1) * size] = block[:, t * 128 : (t + 1) * 128]
    rest = rows * PIECES - count * size
    for t in range(lanes):
        work[t, count * size :] = jnp.zeros((rest, 128), jnp.float32)
    acc = jnp.zeros((rows, 512), jnp.float32)
    for p in range(PIECES):
        ks = pl.ds(p * PIECE, PIECE)
        x = jnp.concatenate(
            [work[t, pl.ds(p, rows, stride=PIECES), :] for t in range(lanes)], axis=1
        ).astype(jnp.bfloat16)
        w = jnp.concatenate([r[ks, :] for r in wide], axis=1)
        acc = acc + jnp.dot(x, w, preferred_element_type=jnp.float32)
    gate_proj = jnp.concatenate([acc[:, :128], acc[:, 256:384]], axis=1)
    up_proj = jnp.concatenate([acc[:, 128:256], acc[:, 384:]], axis=1)
    hidden = (gate_proj / (1.0 + jnp.exp(-gate_proj)) * up_proj).astype(jnp.bfloat16)
    for p in range(PIECES):
        ks = pl.ds(p * PIECE, PIECE)
        out = jnp.dot(hidden, down[:, ks], preferred_element_type=jnp.float32)
        for t in range(lanes):
            work[t, pl.ds(p, rows, stride=PIECES), :] = out[:, t * 128 : (t + 1) * 128]
    for i, ref in enumerate(outs):
        for t in range(lanes):
            part = work[t, i * size : (i + 1) * size]
            ref[:, t * 128 : (t + 1) * 128] = part.astype(jnp.bfloat16)


def experts(blocks, *weights):
    count = len(blocks)
    rows = -(-count * 4 * CAP // 16) * 16
    return pl.pallas_call(
        functools.partial(expert_kernel, count, rows),
        out_shape=(BLOCK,) * count,
        in_specs=[VMEM] * (count + 3),
        out_specs=(VMEM,) * count,
        scratch_shapes=[pltpu.VMEM((PIECE // 128, rows * PIECES, 128), jnp.float32)],
        cost_estimate=pl.CostEstimate(
            flops=2 * rows * WIDTH * 768,
            bytes_accessed=2 * WIDTH * (768 + 2 * rows),
            transcendentals=rows * 256,
        ),
        compiler_params=limit(32),
    )(*blocks, *weights)


def attend_kernel(length_ref, q_hbm, cache_hbm, out_ref, q_ref, cache_ref, sems):
    parts, _, size = cache_ref.shape
    heads = q_ref.shape[1]
    copies = [pltpu.make_async_copy(q_hbm.at[0], q_ref, sems.at[parts])]
    for part in range(parts):
        copies.append(
            pltpu.make_async_copy(
                cache_hbm.at[0, :, pl.ds(part * size, size)], cache_ref.at[part], sems.at[part]
            )
        )
    for copy in copies:
        copy.start()
    copies[0].wait()
    peak = jnp.full((heads, 1), -1e30, jnp.float32)
    total = jnp.zeros((heads, 1), jnp.float32)
    acc = jnp.zeros((heads, LATENT), jnp.float32)
    query = q_ref[...]
    for part in range(parts):
        copies[part + 1].wait()
        scores = (
            lax.dot_general(
                query,
                cache_ref[part],
                (((0,), (0,)), ((), ())),
                preferred_element_type=jnp.float32,
            )
            * score_scale
        )
        at = part * size + lax.broadcasted_iota(jnp.int32, scores.shape, 1)
        scores = jnp.where(at < length_ref[0], scores, jnp.float32(-1e30))
        new = jnp.maximum(peak, jnp.max(scores, axis=1, keepdims=True))
        powered = jnp.exp(scores - new)
        fade = jnp.exp(peak - new)
        total = total * fade + jnp.sum(powered, axis=1, keepdims=True)
        peak = new
        acc = acc * fade + lax.dot_general(
            powered.astype(jnp.bfloat16),
            cache_ref[part, :LATENT],
            (((1,), (1,)), ((), ())),
            preferred_element_type=jnp.float32,
        )
    out_ref[0] = (acc / total).astype(jnp.bfloat16)


def attend(queries, latent_cache, cache_lengths):
    heads, width = queries.shape[1:]
    length = latent_cache.shape[1]
    parts = 4
    return pl.pallas_call(
        attend_kernel,
        out_shape=jax.ShapeDtypeStruct((1, heads, LATENT), jnp.bfloat16),
        in_specs=[
            pl.BlockSpec(memory_space=pltpu.SMEM),
            pl.BlockSpec(memory_space=pltpu.HBM),
            pl.BlockSpec(memory_space=pltpu.HBM),
        ],
        out_specs=pl.BlockSpec(memory_space=pltpu.VMEM),
        scratch_shapes=[
            pltpu.VMEM((width, heads), jnp.bfloat16),
            pltpu.VMEM((parts, width, length // parts), jnp.bfloat16),
            pltpu.SemaphoreType.DMA((parts + 1,)),
        ],
        cost_estimate=pl.CostEstimate(
            flops=2 * heads * length * (width + LATENT),
            bytes_accessed=2 * length * width,
            transcendentals=heads * length,
        ),
        compiler_params=limit(60),
    )(cache_lengths, jnp.swapaxes(queries, 1, 2), jnp.swapaxes(latent_cache, 1, 2))


def local(
    queries,
    latent_cache,
    cache_lengths,
    stream,
    norm_gain,
    expert_ids,
    route_weights,
    w_gate,
    w_up,
    w_down,
):
    *packed, table = pack(stream, norm_gain[None, :], expert_ids, route_weights)
    down_own = w_down[0]
    down_other = swap_core(down_own)
    arrived = [spread(packed[k], k, 1) for k in range(4)]

    wide_own = jnp.concatenate([w_gate[0], w_up[0]], axis=1)
    mine = join(arrived)
    mine, down_own, down_other, wide_own = lax.optimization_barrier(
        (mine, down_own, down_other, wide_own)
    )
    wide_other = swap_core(wide_own)
    down = jnp.concatenate([down_own, down_other], axis=0)

    def over(value):
        return send(value, lambda xl, c, xh, z, y: (1 - xl, c, xh, z, y))

    def along(value, dy):
        return send(value, lambda xl, c, xh, z, y: (xl, c, xh, z, y + dy))

    x_in = over(mine)
    up_in = along(mine, 1)
    dn_in = along(mine, -1)
    y2_in = along(mine, 2)
    x_in, y2_in, wide_other, down = lax.optimization_barrier((x_in, y2_in, wide_other, down))
    weights = (wide_own, wide_other, down)
    x_up_in = along(x_in, 1)
    x_dn_in = along(x_in, -1)
    x_y2_in = over(y2_in)
    own, x_out, y2_out, up_out, dn_out = experts([mine, x_in, y2_in, up_in, dn_in], *weights)
    x_up_in, own = lax.optimization_barrier((x_up_in, own))
    x_up_out, x_dn_out, x_y2_out = experts([x_up_in, x_dn_in, x_y2_in], *weights)
    up_back = along(up_out, -1)
    dn_back = along(dn_out, 1)
    x_up_back = along(x_up_out, -1)
    x_dn_back = along(x_dn_out, 1)
    x_y2_back = over(x_y2_out)

    def add(*values):
        return sum(v.astype(jnp.float32) for v in values)

    near = add(own, up_back, dn_back)
    x_sum = add(x_out, x_up_back, x_dn_back).astype(jnp.bfloat16)
    y2_sum = add(y2_out, x_y2_back).astype(jnp.bfloat16)
    near, x_sum, y2_sum, queries = lax.optimization_barrier((near, x_sum, y2_sum, queries))
    x_back = over(x_sum)
    y2_back = along(y2_sum, 2)
    context = attend(queries, latent_cache, cache_lengths)
    near, context = lax.optimization_barrier((near, context))
    back = split((near, y2_back, x_back))
    returned = [spread(back[k], k, -1) for k in range(4)]
    part = weigh(table, returned)
    pair = part.astype(jnp.float32) + swap_core(part).astype(jnp.float32)
    pair = pair.astype(jnp.bfloat16)
    far = over(pair)
    full = pair.astype(jnp.float32) + far.astype(jnp.float32)
    mixed = (stream.astype(jnp.float32) + full).astype(jnp.bfloat16)
    return (context, mixed)


def solution(mesh):
    return jax.shard_map(
        local,
        mesh=mesh,
        in_specs=(
            P(("sec", "dev"), None, None),
            P(("sec", "dev"), None, None),
            P(("sec", "dev")),
            P("dev", None),
            P(),
            P("dev", None),
            P("dev", None),
            P("dev", None, "sec"),
            P("dev", None, "sec"),
            P("dev", "sec", None),
        ),
        out_specs=(P(("sec", "dev"), None, None), P("dev", None)),
        check_vma=False,
    )
```

```python
import functools

import jax
import jax.numpy as jnp
from jax import lax
from jax.experimental import pallas as pl
from jax.experimental.pallas import tpu as pltpu
from jax.sharding import PartitionSpec as P

LATENT = 512
CAP = 5
ROWS = 8
WIDTH = 7168
PIECES = 8
PIECE = 896
score_scale = 192.0 ** (-0.5)

SIZES = (2, 2, 2, 8, 4)


def pairs(move):
    out = []
    for xl in range(2):
        for c in range(2):
            for xh in range(2):
                for z in range(8):
                    for y in range(4):
                        place = (xl, c, xh, z, y)
                        lin = []
                        for spot in (place, move(*place)):
                            at = 0
                            for part, size in zip(spot, SIZES):
                                at = at * size + part % size
                            lin.append(at)
                        out.append(tuple(lin))
    return out


def send(value, move):
    return lax.ppermute(value, ("sec", "dev"), pairs(move))


def swap_core(value):
    return send(value, lambda xl, c, xh, z, y: (xl, 1 - c, xh, z, y))


STEPS = ((3, -2, 1, 0), (-3, 4, 2, -1))


def spread(value, k, sign):
    def move(xl, c, xh, z, y):
        z = z + sign * STEPS[c][k]
        if xl == xh:
            return (xl, c, xh, z, y)
        return (1 - xl, c, 1 - xh, z, y)

    return send(value, move)


ORDER = (0, 1, 2, 3)


VMEM = pl.BlockSpec(memory_space=pltpu.VMEM)
PACKED = jax.ShapeDtypeStruct((CAP * PIECES, PIECE), jnp.bfloat16)
BLOCK = jax.ShapeDtypeStruct((4 * CAP * PIECES, PIECE), jnp.bfloat16)


def limit(mib):
    return pltpu.CompilerParams(vmem_limit_bytes=mib * 1024 * 1024)


def targets():
    sec, dev = lax.axis_index("sec"), lax.axis_index("dev")
    xl, core = sec // 2, sec % 2
    xh, z = dev // 32, (dev // 4) % 8
    half = jnp.where(xl == xh, xh, 1 - xh) * 8
    steps = [jnp.where(core == 0, STEPS[0][k], STEPS[1][k]) for k in range(4)]
    return [half + (z + step + 8) % 8 for step in steps]


def pack_kernel(*refs):
    sources, (o0, o1, o2, o3, table_ref) = refs[:4], refs[4:9]
    scratch, sems = refs[9:13], refs[13]
    copies = [
        pltpu.make_async_copy(a, b, sems.at[i]) for i, (a, b) in enumerate(zip(sources, scratch))
    ]
    for copy in copies:
        copy.start()
    for copy in copies:
        copy.wait()
    stream_ref, gain_ref, ids_ref, route_ref = scratch
    lane = lax.broadcasted_iota(jnp.int32, (ROWS, 256), 1)
    target, slot, piece = lane // (CAP * PIECES), (lane // PIECES) % CAP, lane % PIECES
    wanted = jnp.full((ROWS, 256), -1, jnp.int32)
    for k, expert in enumerate(targets()):
        wanted = jnp.where(target == k, expert, wanted)
    named = jnp.zeros((ROWS, 256), jnp.float32)
    weight = jnp.zeros((ROWS, 256), jnp.float32)
    ids, route = ids_ref[...], route_ref[...]
    for t in range(ids.shape[1]):
        same = (ids[:, t : t + 1] == wanted).astype(jnp.float32)
        named = named + same
        weight = weight + same * route[:, t : t + 1]
    row = lax.broadcasted_iota(jnp.int32, (ROWS, ROWS), 0)
    col = lax.broadcasted_iota(jnp.int32, (ROWS, ROWS), 1)
    before = jnp.dot((col < row).astype(jnp.float32), named, preferred_element_type=jnp.float32)
    hit = jnp.where(jnp.abs(before - slot.astype(jnp.float32)) < 0.5, named, 0.0)
    table_ref[...] = hit * weight
    picked = jnp.concatenate([jnp.where(piece == p, hit, 0.0) for p in range(PIECES)], axis=0)
    x = stream_ref[...].astype(jnp.float32)
    scale = lax.rsqrt(jnp.sum(x * x, axis=1, keepdims=True) / WIDTH + 1e-06)
    normed = x * scale * gain_ref[...]
    normed = jnp.concatenate(
        [normed[:, p * PIECE : (p + 1) * PIECE] for p in range(PIECES)], axis=0
    )
    out = lax.dot_general(
        picked.astype(jnp.bfloat16),
        normed.astype(jnp.bfloat16),
        (((0,), (0,)), ((), ())),
        preferred_element_type=jnp.float32,
    )
    for k, ref in enumerate((o0, o1, o2, o3)):
        ref[...] = out[k * CAP * PIECES : (k + 1) * CAP * PIECES].astype(jnp.bfloat16)


def pack(stream, gain, ids, route):
    return pl.pallas_call(
        pack_kernel,
        out_shape=(PACKED,) * 4 + (jax.ShapeDtypeStruct((ROWS, 256), jnp.float32),),
        in_specs=[pl.BlockSpec(memory_space=pl.ANY)] * 4,
        out_specs=(VMEM,) * 5,
        scratch_shapes=[pltpu.VMEM(v.shape, v.dtype) for v in (stream, gain, ids, route)]
        + [pltpu.SemaphoreType.DMA((4,))],
        compiler_params=limit(60),
    )(stream, gain, ids, route)


def join_kernel(a, b, c, d, out):
    rows = [ref[...].astype(jnp.float32) for ref in (a, b, c, d)]
    out[...] = jnp.concatenate(rows, axis=0).astype(jnp.bfloat16)


def join(parts):
    return pl.pallas_call(
        join_kernel, out_shape=BLOCK, in_specs=[VMEM] * 4, out_specs=VMEM, compiler_params=limit(8)
    )(*parts)


def split_kernel(b0, b1, b2, o0, o1, o2, o3):
    total = b0[...]
    for ref in (b1, b2):
        total = total + ref[...].astype(jnp.float32)
    for k, ref in enumerate((o0, o1, o2, o3)):
        ref[...] = total[k * CAP * PIECES : (k + 1) * CAP * PIECES].astype(jnp.bfloat16)


def split(blocks):
    return pl.pallas_call(
        split_kernel,
        out_shape=(PACKED,) * 4,
        in_specs=[VMEM] * 3,
        out_specs=(VMEM,) * 4,
        compiler_params=limit(8),
    )(*blocks)


def weigh_kernel(table_ref, a, b, c, d, out):
    rows = [ref[...].astype(jnp.float32) for ref in (a, b, c, d)]
    rows.append(jnp.zeros((256 - 4 * CAP * PIECES, PIECE), jnp.float32))
    rows = jnp.concatenate(rows, axis=0).astype(jnp.bfloat16)
    left = table_ref[...]
    parts = []
    for _ in range(3):
        part = left.astype(jnp.bfloat16).astype(jnp.float32)
        parts.append(part)
        left = left - part
    parts = jnp.concatenate(parts, axis=0)
    piece = lax.broadcasted_iota(jnp.int32, parts.shape, 1) % PIECES
    lhs = jnp.concatenate([jnp.where(piece == p, parts, 0.0) for p in range(PIECES)], axis=0)
    sums = jnp.dot(lhs.astype(jnp.bfloat16), rows, preferred_element_type=jnp.float32)
    for p in range(PIECES):
        at = p * 3 * ROWS
        total = sums[at : at + ROWS]
        total = total + sums[at + ROWS : at + 2 * ROWS] + sums[at + 2 * ROWS : at + 3 * ROWS]
        out[:, p * PIECE : (p + 1) * PIECE] = total.astype(jnp.bfloat16)


def weigh(table, parts):
    return pl.pallas_call(
        weigh_kernel,
        out_shape=jax.ShapeDtypeStruct((ROWS, WIDTH), jnp.bfloat16),
        in_specs=[VMEM] * 5,
        out_specs=VMEM,
        compiler_params=limit(8),
    )(table, *parts)


def expert_kernel(count, rows, *refs):
    blocks = refs[:count]
    wide = refs[count : count + 2]
    down = refs[count + 2]
    outs = refs[count + 3 : -1]
    work = refs[-1]
    size = 4 * CAP * PIECES
    lanes = work.shape[0]
    for i, ref in enumerate(blocks):
        block = ref[...].astype(jnp.float32)
        for t in range(lanes):
            work[t, i * size : (i + 1) * size] = block[:, t * 128 : (t + 1) * 128]
    rest = rows * PIECES - count * size
    for t in range(lanes):
        work[t, count * size :] = jnp.zeros((rest, 128), jnp.float32)
    acc = jnp.zeros((rows, 512), jnp.float32)
    for p in range(PIECES):
        ks = pl.ds(p * PIECE, PIECE)
        x = jnp.concatenate(
            [work[t, pl.ds(p, rows, stride=PIECES), :] for t in range(lanes)], axis=1
        ).astype(jnp.bfloat16)
        w = jnp.concatenate([r[ks, :] for r in wide], axis=1)
        acc = acc + jnp.dot(x, w, preferred_element_type=jnp.float32)
    gate_proj = jnp.concatenate([acc[:, :128], acc[:, 256:384]], axis=1)
    up_proj = jnp.concatenate([acc[:, 128:256], acc[:, 384:]], axis=1)
    hidden = (gate_proj / (1.0 + jnp.exp(-gate_proj)) * up_proj).astype(jnp.bfloat16)
    for p in range(PIECES):
        ks = pl.ds(p * PIECE, PIECE)
        out = jnp.dot(hidden, down[:, ks], preferred_element_type=jnp.float32)
        for t in range(lanes):
            work[t, pl.ds(p, rows, stride=PIECES), :] = out[:, t * 128 : (t + 1) * 128]
    for i, ref in enumerate(outs):
        for t in range(lanes):
            part = work[t, i * size : (i + 1) * size]
            ref[:, t * 128 : (t + 1) * 128] = part.astype(jnp.bfloat16)


def experts(blocks, *weights):
    count = len(blocks)
    rows = -(-count * 4 * CAP // 16) * 16
    return pl.pallas_call(
        functools.partial(expert_kernel, count, rows),
        out_shape=(BLOCK,) * count,
        in_specs=[VMEM] * (count + 3),
        out_specs=(VMEM,) * count,
        scratch_shapes=[pltpu.VMEM((PIECE // 128, rows * PIECES, 128), jnp.float32)],
        cost_estimate=pl.CostEstimate(
            flops=2 * rows * WIDTH * 768,
            bytes_accessed=2 * WIDTH * (768 + 2 * rows),
            transcendentals=rows * 256,
        ),
        compiler_params=limit(32),
    )(*blocks, *weights)


def attend_kernel(length_ref, q_hbm, cache_hbm, out_ref, q_ref, cache_ref, sems):
    parts, _, size = cache_ref.shape
    heads = q_ref.shape[1]
    copies = [pltpu.make_async_copy(q_hbm.at[0], q_ref, sems.at[parts])]
    for part in range(parts):
        copies.append(
            pltpu.make_async_copy(
                cache_hbm.at[0, :, pl.ds(part * size, size)], cache_ref.at[part], sems.at[part]
            )
        )
    for copy in copies:
        copy.start()
    copies[0].wait()
    peak = jnp.full((heads, 1), -1e30, jnp.float32)
    total = jnp.zeros((heads, 1), jnp.float32)
    acc = jnp.zeros((heads, LATENT), jnp.float32)
    query = q_ref[...]
    for part in range(parts):
        copies[part + 1].wait()
        scores = (
            lax.dot_general(
                query,
                cache_ref[part],
                (((0,), (0,)), ((), ())),
                preferred_element_type=jnp.float32,
            )
            * score_scale
        )
        at = part * size + lax.broadcasted_iota(jnp.int32, scores.shape, 1)
        scores = jnp.where(at < length_ref[0], scores, jnp.float32(-1e30))
        new = jnp.maximum(peak, jnp.max(scores, axis=1, keepdims=True))
        powered = jnp.exp(scores - new)
        fade = jnp.exp(peak - new)
        total = total * fade + jnp.sum(powered, axis=1, keepdims=True)
        peak = new
        acc = acc * fade + lax.dot_general(
            powered.astype(jnp.bfloat16),
            cache_ref[part, :LATENT],
            (((1,), (1,)), ((), ())),
            preferred_element_type=jnp.float32,
        )
    out_ref[0] = (acc / total).astype(jnp.bfloat16)


def attend(queries, latent_cache, cache_lengths):
    heads, width = queries.shape[1:]
    length = latent_cache.shape[1]
    parts = 4
    return pl.pallas_call(
        attend_kernel,
        out_shape=jax.ShapeDtypeStruct((1, heads, LATENT), jnp.bfloat16),
        in_specs=[
            pl.BlockSpec(memory_space=pltpu.SMEM),
            pl.BlockSpec(memory_space=pltpu.HBM),
            pl.BlockSpec(memory_space=pltpu.HBM),
        ],
        out_specs=pl.BlockSpec(memory_space=pltpu.VMEM),
        scratch_shapes=[
            pltpu.VMEM((width, heads), jnp.bfloat16),
            pltpu.VMEM((parts, width, length // parts), jnp.bfloat16),
            pltpu.SemaphoreType.DMA((parts + 1,)),
        ],
        cost_estimate=pl.CostEstimate(
            flops=2 * heads * length * (width + LATENT),
            bytes_accessed=2 * length * width,
            transcendentals=heads * length,
        ),
        compiler_params=limit(60),
    )(cache_lengths, jnp.swapaxes(queries, 1, 2), jnp.swapaxes(latent_cache, 1, 2))


def local(
    queries,
    latent_cache,
    cache_lengths,
    stream,
    norm_gain,
    expert_ids,
    route_weights,
    w_gate,
    w_up,
    w_down,
):
    *packed, table = pack(stream, norm_gain[None, :], expert_ids, route_weights)
    down_own = w_down[0]
    down_other = swap_core(down_own)
    arrived = [spread(packed[k], k, 1) for k in range(4)]

    wide_own = jnp.concatenate([w_gate[0], w_up[0]], axis=1)
    mine = join(arrived)
    mine, down_own, down_other, wide_own = lax.optimization_barrier(
        (mine, down_own, down_other, wide_own)
    )
    wide_other = swap_core(wide_own)
    down = jnp.concatenate([down_own, down_other], axis=0)

    def over(value):
        return send(value, lambda xl, c, xh, z, y: (1 - xl, c, xh, z, y))

    def along(value, dy):
        return send(value, lambda xl, c, xh, z, y: (xl, c, xh, z, y + dy))

    x_in = over(mine)
    up_in = along(mine, 1)
    dn_in = along(mine, -1)
    y2_in = along(mine, 2)
    x_in, y2_in, wide_other, down = lax.optimization_barrier((x_in, y2_in, wide_other, down))
    weights = (wide_own, wide_other, down)
    x_up_in = along(x_in, 1)
    x_dn_in = along(x_in, -1)
    x_y2_in = over(y2_in)
    own, x_out, y2_out, up_out, dn_out = experts([mine, x_in, y2_in, up_in, dn_in], *weights)
    x_up_in, own = lax.optimization_barrier((x_up_in, own))
    x_up_out, x_dn_out, x_y2_out = experts([x_up_in, x_dn_in, x_y2_in], *weights)
    up_back = along(up_out, -1)
    dn_back = along(dn_out, 1)
    x_up_back = along(x_up_out, -1)
    x_dn_back = along(x_dn_out, 1)
    x_y2_back = over(x_y2_out)

    def add(*values):
        return sum(v.astype(jnp.float32) for v in values)

    near = add(own, up_back, dn_back)
    x_sum = add(x_out, x_up_back, x_dn_back).astype(jnp.bfloat16)
    y2_sum = add(y2_out, x_y2_back).astype(jnp.bfloat16)
    near, x_sum, y2_sum, queries = lax.optimization_barrier((near, x_sum, y2_sum, queries))
    x_back = over(x_sum)
    y2_back = along(y2_sum, 2)
    context = attend(queries, latent_cache, cache_lengths)
    near, context = lax.optimization_barrier((near, context))
    back = split((near, y2_back, x_back))
    returned = [spread(back[k], k, -1) for k in range(4)]
    part = weigh(table, returned)
    pair = part.astype(jnp.float32) + swap_core(part).astype(jnp.float32)
    pair = pair.astype(jnp.bfloat16)
    far = over(pair)
    full = pair.astype(jnp.float32) + far.astype(jnp.float32)
    mixed = (stream.astype(jnp.float32) + full).astype(jnp.bfloat16)
    return (context, mixed)


def solution(mesh):
    return jax.shard_map(
        local,
        mesh=mesh,
        in_specs=(
            P(("sec", "dev"), None, None),
            P(("sec", "dev"), None, None),
            P(("sec", "dev")),
            P("dev", None),
            P(),
            P("dev", None),
            P("dev", None),
            P("dev", None, "sec"),
            P("dev", None, "sec"),
            P("dev", "sec", None),
        ),
        out_specs=(P(("sec", "dev"), None, None), P("dev", None)),
        check_vma=False,
    )
```

```python
import functools

import jax
import jax.numpy as jnp
from jax import lax
from jax.experimental import pallas as pl
from jax.experimental.pallas import tpu as pltpu
from jax.sharding import PartitionSpec as P

LATENT = 512
CAP = 5
ROWS = 8
WIDTH = 7168
PIECES = 8
PIECE = 896
score_scale = 192.0 ** (-0.5)

SIZES = (2, 2, 2, 8, 4)


def pairs(move):
    out = []
    for xl in range(2):
        for c in range(2):
            for xh in range(2):
                for z in range(8):
                    for y in range(4):
                        place = (xl, c, xh, z, y)
                        lin = []
                        for spot in (place, move(*place)):
                            at = 0
                            for part, size in zip(spot, SIZES):
                                at = at * size + part % size
                            lin.append(at)
                        out.append(tuple(lin))
    return out


def send(value, move):
    return lax.ppermute(value, ("sec", "dev"), pairs(move))


def swap_core(value):
    return send(value, lambda xl, c, xh, z, y: (xl, 1 - c, xh, z, y))


STEPS = ((3, -2, 1, 0), (-3, 4, 2, -1))


def spread(value, k, sign):
    def move(xl, c, xh, z, y):
        z = z + sign * STEPS[c][k]
        if xl == xh:
            return (xl, c, xh, z, y)
        return (1 - xl, c, 1 - xh, z, y)

    return send(value, move)


ORDER = (0, 1, 2, 3)


VMEM = pl.BlockSpec(memory_space=pltpu.VMEM)
PACKED = jax.ShapeDtypeStruct((CAP * PIECES, PIECE), jnp.bfloat16)
BLOCK = jax.ShapeDtypeStruct((4 * CAP * PIECES, PIECE), jnp.bfloat16)


def limit(mib):
    return pltpu.CompilerParams(vmem_limit_bytes=mib * 1024 * 1024)


def targets():
    sec, dev = lax.axis_index("sec"), lax.axis_index("dev")
    xl, core = sec // 2, sec % 2
    xh, z = dev // 32, (dev // 4) % 8
    half = jnp.where(xl == xh, xh, 1 - xh) * 8
    steps = [jnp.where(core == 0, STEPS[0][k], STEPS[1][k]) for k in range(4)]
    return [half + (z + step + 8) % 8 for step in steps]


def pack_kernel(*refs):
    sources, (o0, o1, o2, o3, table_ref) = refs[:4], refs[4:9]
    scratch, sems = refs[9:13], refs[13]
    copies = [
        pltpu.make_async_copy(a, b, sems.at[i]) for i, (a, b) in enumerate(zip(sources, scratch))
    ]
    for copy in copies:
        copy.start()
    for copy in copies:
        copy.wait()
    stream_ref, gain_ref, ids_ref, route_ref = scratch
    lane = lax.broadcasted_iota(jnp.int32, (ROWS, 256), 1)
    target, slot, piece = lane // (CAP * PIECES), (lane // PIECES) % CAP, lane % PIECES
    wanted = jnp.full((ROWS, 256), -1, jnp.int32)
    for k, expert in enumerate(targets()):
        wanted = jnp.where(target == k, expert, wanted)
    named = jnp.zeros((ROWS, 256), jnp.float32)
    weight = jnp.zeros((ROWS, 256), jnp.float32)
    ids, route = ids_ref[...], route_ref[...]
    for t in range(ids.shape[1]):
        same = (ids[:, t : t + 1] == wanted).astype(jnp.float32)
        named = named + same
        weight = weight + same * route[:, t : t + 1]
    row = lax.broadcasted_iota(jnp.int32, (ROWS, ROWS), 0)
    col = lax.broadcasted_iota(jnp.int32, (ROWS, ROWS), 1)
    before = jnp.dot((col < row).astype(jnp.float32), named, preferred_element_type=jnp.float32)
    hit = jnp.where(jnp.abs(before - slot.astype(jnp.float32)) < 0.5, named, 0.0)
    table_ref[...] = hit * weight
    picked = jnp.concatenate([jnp.where(piece == p, hit, 0.0) for p in range(PIECES)], axis=0)
    x = stream_ref[...].astype(jnp.float32)
    scale = lax.rsqrt(jnp.sum(x * x, axis=1, keepdims=True) / WIDTH + 1e-06)
    normed = x * scale * gain_ref[...]
    normed = jnp.concatenate(
        [normed[:, p * PIECE : (p + 1) * PIECE] for p in range(PIECES)], axis=0
    )
    out = lax.dot_general(
        picked.astype(jnp.bfloat16),
        normed.astype(jnp.bfloat16),
        (((0,), (0,)), ((), ())),
        preferred_element_type=jnp.float32,
    )
    for k, ref in enumerate((o0, o1, o2, o3)):
        ref[...] = out[k * CAP * PIECES : (k + 1) * CAP * PIECES].astype(jnp.bfloat16)


def pack(stream, gain, ids, route):
    return pl.pallas_call(
        pack_kernel,
        out_shape=(PACKED,) * 4 + (jax.ShapeDtypeStruct((ROWS, 256), jnp.float32),),
        in_specs=[pl.BlockSpec(memory_space=pl.ANY)] * 4,
        out_specs=(VMEM,) * 5,
        scratch_shapes=[pltpu.VMEM(v.shape, v.dtype) for v in (stream, gain, ids, route)]
        + [pltpu.SemaphoreType.DMA((4,))],
        compiler_params=limit(60),
    )(stream, gain, ids, route)


def join_kernel(a, b, c, d, out):
    rows = [ref[...].astype(jnp.float32) for ref in (a, b, c, d)]
    out[...] = jnp.concatenate(rows, axis=0).astype(jnp.bfloat16)


def join(parts):
    return pl.pallas_call(
        join_kernel, out_shape=BLOCK, in_specs=[VMEM] * 4, out_specs=VMEM, compiler_params=limit(8)
    )(*parts)


def split_kernel(b0, b1, o0, o1, o2, o3):
    total = b0[...] + b1[...].astype(jnp.float32)
    for k, ref in enumerate((o0, o1, o2, o3)):
        ref[...] = total[k * CAP * PIECES : (k + 1) * CAP * PIECES].astype(jnp.bfloat16)


def split(blocks):
    return pl.pallas_call(
        split_kernel,
        out_shape=(PACKED,) * 4,
        in_specs=[VMEM] * 2,
        out_specs=(VMEM,) * 4,
        compiler_params=limit(8),
    )(*blocks)


def weigh_kernel(table_ref, a, b, c, d, out):
    rows = [ref[...].astype(jnp.float32) for ref in (a, b, c, d)]
    rows.append(jnp.zeros((256 - 4 * CAP * PIECES, PIECE), jnp.float32))
    rows = jnp.concatenate(rows, axis=0).astype(jnp.bfloat16)
    left = table_ref[...]
    parts = []
    for _ in range(3):
        part = left.astype(jnp.bfloat16).astype(jnp.float32)
        parts.append(part)
        left = left - part
    parts = jnp.concatenate(parts, axis=0)
    piece = lax.broadcasted_iota(jnp.int32, parts.shape, 1) % PIECES
    lhs = jnp.concatenate([jnp.where(piece == p, parts, 0.0) for p in range(PIECES)], axis=0)
    sums = jnp.dot(lhs.astype(jnp.bfloat16), rows, preferred_element_type=jnp.float32)
    for p in range(PIECES):
        at = p * 3 * ROWS
        total = sums[at : at + ROWS]
        total = total + sums[at + ROWS : at + 2 * ROWS] + sums[at + 2 * ROWS : at + 3 * ROWS]
        out[:, p * PIECE : (p + 1) * PIECE] = total.astype(jnp.bfloat16)


def weigh(table, parts):
    return pl.pallas_call(
        weigh_kernel,
        out_shape=jax.ShapeDtypeStruct((ROWS, WIDTH), jnp.bfloat16),
        in_specs=[VMEM] * 5,
        out_specs=VMEM,
        compiler_params=limit(8),
    )(table, *parts)


def expert_kernel(count, rows, *refs):
    blocks = refs[:count]
    wide = refs[count : count + 2]
    down = refs[count + 2]
    outs = refs[count + 3 : -1]
    work = refs[-1]
    size = 4 * CAP * PIECES
    lanes = work.shape[0]
    for i, ref in enumerate(blocks):
        block = ref[...].astype(jnp.float32)
        for t in range(lanes):
            work[t, i * size : (i + 1) * size] = block[:, t * 128 : (t + 1) * 128]
    rest = rows * PIECES - count * size
    for t in range(lanes):
        work[t, count * size :] = jnp.zeros((rest, 128), jnp.float32)
    acc = jnp.zeros((rows, 512), jnp.float32)
    for p in range(PIECES):
        ks = pl.ds(p * PIECE, PIECE)
        x = jnp.concatenate(
            [work[t, pl.ds(p, rows, stride=PIECES), :] for t in range(lanes)], axis=1
        ).astype(jnp.bfloat16)
        w = jnp.concatenate([r[ks, :] for r in wide], axis=1)
        acc = acc + jnp.dot(x, w, preferred_element_type=jnp.float32)
    gate_proj = jnp.concatenate([acc[:, :128], acc[:, 256:384]], axis=1)
    up_proj = jnp.concatenate([acc[:, 128:256], acc[:, 384:]], axis=1)
    hidden = (gate_proj / (1.0 + jnp.exp(-gate_proj)) * up_proj).astype(jnp.bfloat16)
    for p in range(PIECES):
        ks = pl.ds(p * PIECE, PIECE)
        out = jnp.dot(hidden, down[:, ks], preferred_element_type=jnp.float32)
        for t in range(lanes):
            work[t, pl.ds(p, rows, stride=PIECES), :] = out[:, t * 128 : (t + 1) * 128]
    for i, ref in enumerate(outs):
        for t in range(lanes):
            part = work[t, i * size : (i + 1) * size]
            ref[:, t * 128 : (t + 1) * 128] = part.astype(jnp.bfloat16)


def experts(blocks, *weights):
    count = len(blocks)
    rows = -(-count * 4 * CAP // 16) * 16
    return pl.pallas_call(
        functools.partial(expert_kernel, count, rows),
        out_shape=(BLOCK,) * count,
        in_specs=[VMEM] * (count + 3),
        out_specs=(VMEM,) * count,
        scratch_shapes=[pltpu.VMEM((PIECE // 128, rows * PIECES, 128), jnp.float32)],
        cost_estimate=pl.CostEstimate(
            flops=2 * rows * WIDTH * 768,
            bytes_accessed=2 * WIDTH * (768 + 2 * rows),
            transcendentals=rows * 256,
        ),
        compiler_params=limit(32),
    )(*blocks, *weights)


def attend_kernel(length_ref, q_hbm, cache_hbm, out_ref, q_ref, cache_ref, sems):
    parts, _, size = cache_ref.shape
    heads = q_ref.shape[1]
    copies = [pltpu.make_async_copy(q_hbm.at[0], q_ref, sems.at[parts])]
    for part in range(parts):
        copies.append(
            pltpu.make_async_copy(
                cache_hbm.at[0, :, pl.ds(part * size, size)], cache_ref.at[part], sems.at[part]
            )
        )
    for copy in copies:
        copy.start()
    copies[0].wait()
    peak = jnp.full((heads, 1), -1e30, jnp.float32)
    total = jnp.zeros((heads, 1), jnp.float32)
    acc = jnp.zeros((heads, LATENT), jnp.float32)
    query = q_ref[...]
    for part in range(parts):
        copies[part + 1].wait()
        scores = (
            lax.dot_general(
                query,
                cache_ref[part],
                (((0,), (0,)), ((), ())),
                preferred_element_type=jnp.float32,
            )
            * score_scale
        )
        at = part * size + lax.broadcasted_iota(jnp.int32, scores.shape, 1)
        scores = jnp.where(at < length_ref[0], scores, jnp.float32(-1e30))
        new = jnp.maximum(peak, jnp.max(scores, axis=1, keepdims=True))
        powered = jnp.exp(scores - new)
        fade = jnp.exp(peak - new)
        total = total * fade + jnp.sum(powered, axis=1, keepdims=True)
        peak = new
        acc = acc * fade + lax.dot_general(
            powered.astype(jnp.bfloat16),
            cache_ref[part, :LATENT],
            (((1,), (1,)), ((), ())),
            preferred_element_type=jnp.float32,
        )
    out_ref[0] = (acc / total).astype(jnp.bfloat16)


def attend(queries, latent_cache, cache_lengths):
    heads, width = queries.shape[1:]
    length = latent_cache.shape[1]
    parts = 4
    return pl.pallas_call(
        attend_kernel,
        out_shape=jax.ShapeDtypeStruct((1, heads, LATENT), jnp.bfloat16),
        in_specs=[
            pl.BlockSpec(memory_space=pltpu.SMEM),
            pl.BlockSpec(memory_space=pltpu.HBM),
            pl.BlockSpec(memory_space=pltpu.HBM),
        ],
        out_specs=pl.BlockSpec(memory_space=pltpu.VMEM),
        scratch_shapes=[
            pltpu.VMEM((width, heads), jnp.bfloat16),
            pltpu.VMEM((parts, width, length // parts), jnp.bfloat16),
            pltpu.SemaphoreType.DMA((parts + 1,)),
        ],
        cost_estimate=pl.CostEstimate(
            flops=2 * heads * length * (width + LATENT),
            bytes_accessed=2 * length * width,
            transcendentals=heads * length,
        ),
        compiler_params=limit(60),
    )(cache_lengths, jnp.swapaxes(queries, 1, 2), jnp.swapaxes(latent_cache, 1, 2))


def local(
    queries,
    latent_cache,
    cache_lengths,
    stream,
    norm_gain,
    expert_ids,
    route_weights,
    w_gate,
    w_up,
    w_down,
):
    *packed, table = pack(stream, norm_gain[None, :], expert_ids, route_weights)
    down_own = w_down[0]
    down_other = swap_core(down_own)
    arrived = [spread(packed[k], k, 1) for k in range(4)]

    wide_own = jnp.concatenate([w_gate[0], w_up[0]], axis=1)
    mine = join(arrived)
    mine, down_own, down_other, wide_own = lax.optimization_barrier(
        (mine, down_own, down_other, wide_own)
    )
    wide_other = swap_core(wide_own)
    down = jnp.concatenate([down_own, down_other], axis=0)

    def over(value):
        return send(value, lambda xl, c, xh, z, y: (1 - xl, c, xh, z, y))

    def along(value, dy):
        return send(value, lambda xl, c, xh, z, y: (xl, c, xh, z, y + dy))

    x_in = over(mine)
    up_in = along(mine, 1)
    dn_in = along(mine, -1)
    y2_in = along(mine, 2)
    x_in, wide_other, down = lax.optimization_barrier((x_in, wide_other, down))
    y2_in, _ = lax.optimization_barrier((y2_in, x_in))
    weights = (wide_own, wide_other, down)
    x_up_in = along(x_in, 1)
    x_dn_in = along(x_in, -1)
    x_y2_in = over(y2_in)
    own, x_out, y2_out, up_out, dn_out = experts([mine, x_in, y2_in, up_in, dn_in], *weights)
    x_up_in, own = lax.optimization_barrier((x_up_in, own))
    x_up_out, x_dn_out, x_y2_out = experts([x_up_in, x_dn_in, x_y2_in], *weights)
    up_back = along(up_out, -1)
    dn_back = along(dn_out, 1)
    x_up_back = along(x_up_out, -1)
    x_dn_back = along(x_dn_out, 1)
    x_y2_back = over(x_y2_out)

    def add(*values):
        return sum(v.astype(jnp.float32) for v in values)

    near = add(own, up_back, dn_back)
    y2_sum = add(y2_out, x_y2_back).astype(jnp.bfloat16)
    y2_back = along(y2_sum, 2)
    x_up_back, _ = lax.optimization_barrier((x_up_back, y2_sum))
    x_sum = add(x_out, x_up_back, x_dn_back).astype(jnp.bfloat16)
    near, x_sum, queries = lax.optimization_barrier((near, x_sum, queries))
    x_back = over(x_sum)
    context = attend(queries, latent_cache, cache_lengths)
    near, context = lax.optimization_barrier((near, context))
    near = add(near, y2_back)
    back = split((near, x_back))
    returned = [spread(back[k], k, -1) for k in range(4)]
    part = weigh(table, returned)
    pair = part.astype(jnp.float32) + swap_core(part).astype(jnp.float32)
    pair = pair.astype(jnp.bfloat16)
    far = over(pair)
    full = pair.astype(jnp.float32) + far.astype(jnp.float32)
    mixed = (stream.astype(jnp.float32) + full).astype(jnp.bfloat16)
    return (context, mixed)


def solution(mesh):
    return jax.shard_map(
        local,
        mesh=mesh,
        in_specs=(
            P(("sec", "dev"), None, None),
            P(("sec", "dev"), None, None),
            P(("sec", "dev")),
            P("dev", None),
            P(),
            P("dev", None),
            P("dev", None),
            P("dev", None, "sec"),
            P("dev", None, "sec"),
            P("dev", "sec", None),
        ),
        out_specs=(P(("sec", "dev"), None, None), P("dev", None)),
        check_vma=False,
    )
```

```python
import functools

import jax
import jax.numpy as jnp
from jax import lax
from jax.experimental import pallas as pl
from jax.experimental.pallas import tpu as pltpu
from jax.sharding import PartitionSpec as P

LATENT = 512
CAP = 5
ROWS = 8
WIDTH = 7168
PIECES = 8
PIECE = 896
score_scale = 192.0 ** (-0.5)

SIZES = (2, 2, 2, 8, 4)


def pairs(move):
    out = []
    for xl in range(2):
        for c in range(2):
            for xh in range(2):
                for z in range(8):
                    for y in range(4):
                        place = (xl, c, xh, z, y)
                        lin = []
                        for spot in (place, move(*place)):
                            at = 0
                            for part, size in zip(spot, SIZES):
                                at = at * size + part % size
                            lin.append(at)
                        out.append(tuple(lin))
    return out


def send(value, move):
    return lax.ppermute(value, ("sec", "dev"), pairs(move))


def swap_core(value):
    return send(value, lambda xl, c, xh, z, y: (xl, 1 - c, xh, z, y))


STEPS = ((3, -2, 1, 0), (-3, 4, 2, -1))


def spread(value, k, sign):
    def move(xl, c, xh, z, y):
        z = z + sign * STEPS[c][k]
        if xl == xh:
            return (xl, c, xh, z, y)
        return (1 - xl, c, 1 - xh, z, y)

    return send(value, move)


ORDER = (0, 1, 2, 3)


VMEM = pl.BlockSpec(memory_space=pltpu.VMEM)
PACKED = jax.ShapeDtypeStruct((CAP * PIECES, PIECE), jnp.bfloat16)
BLOCK = jax.ShapeDtypeStruct((4 * CAP * PIECES, PIECE), jnp.bfloat16)


def limit(mib):
    return pltpu.CompilerParams(vmem_limit_bytes=mib * 1024 * 1024)


def targets():
    sec, dev = lax.axis_index("sec"), lax.axis_index("dev")
    xl, core = sec // 2, sec % 2
    xh, z = dev // 32, (dev // 4) % 8
    half = jnp.where(xl == xh, xh, 1 - xh) * 8
    steps = [jnp.where(core == 0, STEPS[0][k], STEPS[1][k]) for k in range(4)]
    return [half + (z + step + 8) % 8 for step in steps]


def pack_kernel(*refs):
    sources, (o0, o1, o2, o3, table_ref) = refs[:4], refs[4:9]
    scratch, sems = refs[9:13], refs[13]
    copies = [
        pltpu.make_async_copy(a, b, sems.at[i]) for i, (a, b) in enumerate(zip(sources, scratch))
    ]
    for copy in copies:
        copy.start()
    for copy in copies:
        copy.wait()
    stream_ref, gain_ref, ids_ref, route_ref = scratch
    lane = lax.broadcasted_iota(jnp.int32, (ROWS, 256), 1)
    target, slot, piece = lane // (CAP * PIECES), (lane // PIECES) % CAP, lane % PIECES
    wanted = jnp.full((ROWS, 256), -1, jnp.int32)
    for k, expert in enumerate(targets()):
        wanted = jnp.where(target == k, expert, wanted)
    named = jnp.zeros((ROWS, 256), jnp.float32)
    weight = jnp.zeros((ROWS, 256), jnp.float32)
    ids, route = ids_ref[...], route_ref[...]
    for t in range(ids.shape[1]):
        same = (ids[:, t : t + 1] == wanted).astype(jnp.float32)
        named = named + same
        weight = weight + same * route[:, t : t + 1]
    row = lax.broadcasted_iota(jnp.int32, (ROWS, ROWS), 0)
    col = lax.broadcasted_iota(jnp.int32, (ROWS, ROWS), 1)
    before = jnp.dot((col < row).astype(jnp.float32), named, preferred_element_type=jnp.float32)
    hit = jnp.where(jnp.abs(before - slot.astype(jnp.float32)) < 0.5, named, 0.0)
    table_ref[...] = hit * weight
    picked = jnp.concatenate([jnp.where(piece == p, hit, 0.0) for p in range(PIECES)], axis=0)
    x = stream_ref[...].astype(jnp.float32)
    scale = lax.rsqrt(jnp.sum(x * x, axis=1, keepdims=True) / WIDTH + 1e-06)
    normed = x * scale * gain_ref[...]
    normed = jnp.concatenate(
        [normed[:, p * PIECE : (p + 1) * PIECE] for p in range(PIECES)], axis=0
    )
    out = lax.dot_general(
        picked.astype(jnp.bfloat16),
        normed.astype(jnp.bfloat16),
        (((0,), (0,)), ((), ())),
        preferred_element_type=jnp.float32,
    )
    for k, ref in enumerate((o0, o1, o2, o3)):
        ref[...] = out[k * CAP * PIECES : (k + 1) * CAP * PIECES].astype(jnp.bfloat16)


def pack(stream, gain, ids, route):
    return pl.pallas_call(
        pack_kernel,
        out_shape=(PACKED,) * 4 + (jax.ShapeDtypeStruct((ROWS, 256), jnp.float32),),
        in_specs=[pl.BlockSpec(memory_space=pl.ANY)] * 4,
        out_specs=(VMEM,) * 5,
        scratch_shapes=[pltpu.VMEM(v.shape, v.dtype) for v in (stream, gain, ids, route)]
        + [pltpu.SemaphoreType.DMA((4,))],
        compiler_params=limit(60),
    )(stream, gain, ids, route)


def join_kernel(a, b, c, d, out):
    rows = [ref[...].astype(jnp.float32) for ref in (a, b, c, d)]
    out[...] = jnp.concatenate(rows, axis=0).astype(jnp.bfloat16)


def join(parts):
    return pl.pallas_call(
        join_kernel, out_shape=BLOCK, in_specs=[VMEM] * 4, out_specs=VMEM, compiler_params=limit(8)
    )(*parts)


def split_kernel(b0, b1, o0, o1, o2, o3):
    total = b0[...] + b1[...].astype(jnp.float32)
    for k, ref in enumerate((o0, o1, o2, o3)):
        ref[...] = total[k * CAP * PIECES : (k + 1) * CAP * PIECES].astype(jnp.bfloat16)


def split(blocks):
    return pl.pallas_call(
        split_kernel,
        out_shape=(PACKED,) * 4,
        in_specs=[VMEM] * 2,
        out_specs=(VMEM,) * 4,
        compiler_params=limit(8),
    )(*blocks)


def weigh_kernel(table_ref, a, b, c, d, out):
    rows = [ref[...].astype(jnp.float32) for ref in (a, b, c, d)]
    rows.append(jnp.zeros((256 - 4 * CAP * PIECES, PIECE), jnp.float32))
    rows = jnp.concatenate(rows, axis=0).astype(jnp.bfloat16)
    left = table_ref[...]
    parts = []
    for _ in range(3):
        part = left.astype(jnp.bfloat16).astype(jnp.float32)
        parts.append(part)
        left = left - part
    parts = jnp.concatenate(parts, axis=0)
    piece = lax.broadcasted_iota(jnp.int32, parts.shape, 1) % PIECES
    lhs = jnp.concatenate([jnp.where(piece == p, parts, 0.0) for p in range(PIECES)], axis=0)
    sums = jnp.dot(lhs.astype(jnp.bfloat16), rows, preferred_element_type=jnp.float32)
    for p in range(PIECES):
        at = p * 3 * ROWS
        total = sums[at : at + ROWS]
        total = total + sums[at + ROWS : at + 2 * ROWS] + sums[at + 2 * ROWS : at + 3 * ROWS]
        out[:, p * PIECE : (p + 1) * PIECE] = total.astype(jnp.bfloat16)


def weigh(table, parts):
    return pl.pallas_call(
        weigh_kernel,
        out_shape=jax.ShapeDtypeStruct((ROWS, WIDTH), jnp.bfloat16),
        in_specs=[VMEM] * 5,
        out_specs=VMEM,
        compiler_params=limit(8),
    )(table, *parts)


def expert_kernel(count, rows, *refs):
    blocks = refs[:count]
    wide = refs[count : count + 2]
    down = refs[count + 2]
    outs = refs[count + 3 : -1]
    work = refs[-1]
    size = 4 * CAP * PIECES
    lanes = work.shape[0]
    for i, ref in enumerate(blocks):
        block = ref[...].astype(jnp.float32)
        for t in range(lanes):
            work[t, i * size : (i + 1) * size] = block[:, t * 128 : (t + 1) * 128]
    rest = rows * PIECES - count * size
    for t in range(lanes):
        work[t, count * size :] = jnp.zeros((rest, 128), jnp.float32)
    acc = jnp.zeros((rows, 512), jnp.float32)
    for p in range(PIECES):
        ks = pl.ds(p * PIECE, PIECE)
        x = jnp.concatenate(
            [work[t, pl.ds(p, rows, stride=PIECES), :] for t in range(lanes)], axis=1
        ).astype(jnp.bfloat16)
        w = jnp.concatenate([r[ks, :] for r in wide], axis=1)
        acc = acc + jnp.dot(x, w, preferred_element_type=jnp.float32)
    gate_proj = jnp.concatenate([acc[:, :128], acc[:, 256:384]], axis=1)
    up_proj = jnp.concatenate([acc[:, 128:256], acc[:, 384:]], axis=1)
    hidden = (gate_proj / (1.0 + jnp.exp(-gate_proj)) * up_proj).astype(jnp.bfloat16)
    for p in range(PIECES):
        ks = pl.ds(p * PIECE, PIECE)
        out = jnp.dot(hidden, down[:, ks], preferred_element_type=jnp.float32)
        for t in range(lanes):
            work[t, pl.ds(p, rows, stride=PIECES), :] = out[:, t * 128 : (t + 1) * 128]
    for i, ref in enumerate(outs):
        for t in range(lanes):
            part = work[t, i * size : (i + 1) * size]
            ref[:, t * 128 : (t + 1) * 128] = part.astype(jnp.bfloat16)


def experts(blocks, *weights):
    count = len(blocks)
    rows = -(-count * 4 * CAP // 16) * 16
    return pl.pallas_call(
        functools.partial(expert_kernel, count, rows),
        out_shape=(BLOCK,) * count,
        in_specs=[VMEM] * (count + 3),
        out_specs=(VMEM,) * count,
        scratch_shapes=[pltpu.VMEM((PIECE // 128, rows * PIECES, 128), jnp.float32)],
        cost_estimate=pl.CostEstimate(
            flops=2 * rows * WIDTH * 768,
            bytes_accessed=2 * WIDTH * (768 + 2 * rows),
            transcendentals=rows * 256,
        ),
        compiler_params=limit(32),
    )(*blocks, *weights)


def attend_kernel(length_ref, q_hbm, cache_hbm, out_ref, q_ref, cache_ref, sems):
    parts, _, size = cache_ref.shape
    heads = q_ref.shape[1]
    copies = [pltpu.make_async_copy(q_hbm.at[0], q_ref, sems.at[parts])]
    for part in range(parts):
        copies.append(
            pltpu.make_async_copy(
                cache_hbm.at[0, :, pl.ds(part * size, size)], cache_ref.at[part], sems.at[part]
            )
        )
    for copy in copies:
        copy.start()
    copies[0].wait()
    peak = jnp.full((heads, 1), -1e30, jnp.float32)
    total = jnp.zeros((heads, 1), jnp.float32)
    acc = jnp.zeros((heads, LATENT), jnp.float32)
    query = q_ref[...]
    for part in range(parts):
        copies[part + 1].wait()
        scores = (
            lax.dot_general(
                query,
                cache_ref[part],
                (((0,), (0,)), ((), ())),
                preferred_element_type=jnp.float32,
            )
            * score_scale
        )
        at = part * size + lax.broadcasted_iota(jnp.int32, scores.shape, 1)
        scores = jnp.where(at < length_ref[0:1, 0:1], scores, jnp.float32(-1e30))
        new = jnp.maximum(peak, jnp.max(scores, axis=1, keepdims=True))
        powered = jnp.exp(scores - new)
        fade = jnp.exp(peak - new)
        total = total * fade + jnp.sum(powered, axis=1, keepdims=True)
        peak = new
        acc = acc * fade + lax.dot_general(
            powered.astype(jnp.bfloat16),
            cache_ref[part, :LATENT],
            (((1,), (1,)), ((), ())),
            preferred_element_type=jnp.float32,
        )
    out_ref[0] = (acc / total).astype(jnp.bfloat16)


def attend(queries, latent_cache, cache_lengths):
    heads, width = queries.shape[1:]
    length = latent_cache.shape[1]
    parts = 4
    return pl.pallas_call(
        attend_kernel,
        out_shape=jax.ShapeDtypeStruct((1, heads, LATENT), jnp.bfloat16),
        in_specs=[
            VMEM,
            pl.BlockSpec(memory_space=pltpu.HBM),
            pl.BlockSpec(memory_space=pltpu.HBM),
        ],
        out_specs=pl.BlockSpec(memory_space=pltpu.VMEM),
        scratch_shapes=[
            pltpu.VMEM((width, heads), jnp.bfloat16),
            pltpu.VMEM((parts, width, length // parts), jnp.bfloat16),
            pltpu.SemaphoreType.DMA((parts + 1,)),
        ],
        cost_estimate=pl.CostEstimate(
            flops=2 * heads * length * (width + LATENT),
            bytes_accessed=2 * length * width,
            transcendentals=heads * length,
        ),
        compiler_params=limit(60),
    )(cache_lengths, jnp.swapaxes(queries, 1, 2), jnp.swapaxes(latent_cache, 1, 2))


def local(
    queries,
    latent_cache,
    cache_lengths,
    stream,
    norm_gain,
    expert_ids,
    route_weights,
    w_gate,
    w_up,
    w_down,
):
    *packed, table = pack(stream, norm_gain[None, :], expert_ids, route_weights)
    down_own = w_down[0]
    down_other = swap_core(down_own)
    arrived = [spread(packed[k], k, 1) for k in range(4)]

    wide_own = jnp.concatenate([w_gate[0], w_up[0]], axis=1)
    mine = join(arrived)
    cache_lengths = jnp.broadcast_to(cache_lengths[:, None], (8, 128))
    mine, down_own, down_other, wide_own, cache_lengths = lax.optimization_barrier(
        (mine, down_own, down_other, wide_own, cache_lengths)
    )
    wide_other = swap_core(wide_own)
    down = jnp.concatenate([down_own, down_other], axis=0)

    def over(value):
        return send(value, lambda xl, c, xh, z, y: (1 - xl, c, xh, z, y))

    def along(value, dy):
        return send(value, lambda xl, c, xh, z, y: (xl, c, xh, z, y + dy))

    x_in = over(mine)
    up_in = along(mine, 1)
    dn_in = along(mine, -1)
    y2_in = along(mine, 2)
    x_in, wide_other, down = lax.optimization_barrier((x_in, wide_other, down))
    y2_in, _ = lax.optimization_barrier((y2_in, x_in))
    weights = (wide_own, wide_other, down)
    x_up_in = along(x_in, 1)
    x_dn_in = along(x_in, -1)
    x_y2_in = over(y2_in)
    own, x_out, y2_out, up_out, dn_out = experts([mine, x_in, y2_in, up_in, dn_in], *weights)
    x_up_in, own = lax.optimization_barrier((x_up_in, own))
    x_up_out, x_dn_out, x_y2_out = experts([x_up_in, x_dn_in, x_y2_in], *weights)
    up_back = along(up_out, -1)
    dn_back = along(dn_out, 1)
    x_up_back = along(x_up_out, -1)
    x_dn_back = along(x_dn_out, 1)
    x_y2_back = over(x_y2_out)

    def add(*values):
        return sum(v.astype(jnp.float32) for v in values)

    near = add(own, up_back, dn_back)
    y2_sum = add(y2_out, x_y2_back).astype(jnp.bfloat16)
    y2_back = along(y2_sum, 2)
    x_up_back, _ = lax.optimization_barrier((x_up_back, y2_sum))
    x_sum = add(x_out, x_up_back, x_dn_back).astype(jnp.bfloat16)
    near, x_sum, queries = lax.optimization_barrier((near, x_sum, queries))
    x_back = over(x_sum)
    context = attend(queries, latent_cache, cache_lengths)
    near, context = lax.optimization_barrier((near, context))
    near = add(near, y2_back)
    back = split((near, x_back))
    returned = [spread(back[k], k, -1) for k in range(4)]
    part = weigh(table, returned)
    pair = part.astype(jnp.float32) + swap_core(part).astype(jnp.float32)
    pair = pair.astype(jnp.bfloat16)
    far = over(pair)
    full = pair.astype(jnp.float32) + far.astype(jnp.float32)
    mixed = (stream.astype(jnp.float32) + full).astype(jnp.bfloat16)
    return (context, mixed)


def solution(mesh):
    return jax.shard_map(
        local,
        mesh=mesh,
        in_specs=(
            P(("sec", "dev"), None, None),
            P(("sec", "dev"), None, None),
            P(("sec", "dev")),
            P("dev", None),
            P(),
            P("dev", None),
            P("dev", None),
            P("dev", None, "sec"),
            P("dev", None, "sec"),
            P("dev", "sec", None),
        ),
        out_specs=(P(("sec", "dev"), None, None), P("dev", None)),
        check_vma=False,
    )
```
